512 devices in a mesh: sample: 16 (over z_lo, x), var: 32 (over y, z_hi, core).
Axes of the slice: x: 4, y: 8, z: 8 (z_hi: 2, z_lo: 4; z = z_hi * 4 + z_lo), core: 2. Of those that a mesh axis runs over, the one named last changes fastest.
Arguments:
- data: bfloat16 [12288, 65536], P('sample', 'var'), may hold values from -6 to 6
- test_matrix: bfloat16 [65536, 256], P('var'), may hold values from -6 to 6
Outputs:
- sketch_cov: float32 [65536, 256], P('var', 'sample')
- core_factor: float32 [256, 256], replicated
The draws below stay inside these ranges and needn't reach their ends.
All inputs are finite; a program needn't handle non-finite values.
Results may differ from the reference program's by a relative error of at most 0.0027.
Values may be sent and summed in bfloat16 or wider, within the bound.
A program may use at most 64 MiB of HBM per device.

```python
import math
import jax
import jax.numpy as jnp
from jax import lax

K = 256
VARS = 65536
ROWS = 12288


def shard_levels(key, shape, split, smallest, high):
    level, own = 1.0, jax.random.fold_in(key, 6)
    for axis_at, shards_of in split:
        draws = jnp.exp(jax.random.uniform(jax.random.fold_in(own, axis_at), (shards_of,), jnp.float32, smallest / len(split), high / len(split)))
        level = level * jnp.repeat(draws, shape[axis_at] // shards_of).reshape([-1 if axis == axis_at else 1 for axis in range(len(shape))])
    return level


def normal_values(stream_key, shape, scale, bound, pieces=(), dtype=jnp.bfloat16):
    drawn = scale * jax.random.normal(stream_key, shape, jnp.float32)
    if pieces:
        drawn = drawn * shard_levels(stream_key, shape, pieces, -0.22, 0.18)
    return jnp.clip(drawn, -bound, bound).astype(dtype)


def setup_inputs(seed: int = 0) -> dict:
    keys = jax.random.split(jax.random.key(seed), 3)
    return {
        "data": normal_values(keys[0], (ROWS, VARS), 1.0, 6.0, ((0, 16), (1, 32))),
        "test_matrix": normal_values(keys[1], (VARS, K), 1.0, 6.0, ((0, 32),)),
    }


def reference(data, test_matrix):
    sketch = (jnp.dot(data.astype(jnp.float32), test_matrix.astype(jnp.float32), preferred_element_type=jnp.float32) * (1.0 / math.sqrt(VARS))).astype(jnp.bfloat16)
    sketch_cov = jnp.dot(data.T.astype(jnp.float32), sketch.astype(jnp.float32), preferred_element_type=jnp.float32) * (1.0 / math.sqrt(ROWS))
    core = jnp.dot(test_matrix.astype(jnp.float32).T.astype(jnp.float32), sketch_cov.astype(jnp.float32), precision=lax.Precision.HIGHEST, preferred_element_type=jnp.float32) * (1.0 / math.sqrt(VARS * ROWS))
    core = (core + core.T) * 0.5
    core_factor = jnp.linalg.cholesky(core)
    return (sketch_cov, core_factor)
```

```python
import math

import jax
import jax.numpy as jnp
from jax import lax
from jax.experimental import pallas as pl
from jax.experimental.pallas import tpu as pltpu
from jax.sharding import PartitionSpec as P

MESH = pl.DeviceIdType.MESH
HIGHEST = lax.Precision.HIGHEST
F32 = jnp.float32
BF16 = jnp.bfloat16

NX, NY, NZ = 4, 8, 8
NZL = 4
K = 256
HALF = 128
BLOCK = 16
SLAB = 64


def position():
    s = lax.axis_index("sample")
    v = lax.axis_index("var")
    x = lax.rem(s, NX)
    zl = s // NX
    c = lax.rem(v, 2)
    zh = lax.rem(v // 2, 2)
    y = v // 4
    return x, y, zh * NZL + zl, c


def device(x, y, z, c):
    return (lax.rem(z, NZL) * NX + x, y * 4 + (z // NZL) * 2 + c)


def remote(src, dst, send, recv, target):
    return pltpu.make_async_remote_copy(
        src_ref=src, dst_ref=dst, send_sem=send, recv_sem=recv,
        device_id=target, device_id_type=MESH,
    )


def factor_slab(block, rows, lanes):
    wide = lanes // HALF

    def spread(a):
        return jnp.concatenate([a] * wide, axis=1)

    count = rows // 8
    tiles = [block[8 * t:8 * t + 8, :] for t in range(count)]
    done = []
    row_at = lax.broadcasted_iota(jnp.int32, (8, lanes), 0)
    for t in range(count):
        tile = tiles[t]
        base = 8 * t
        below = range(t + 1, count)
        piv = {}
        for i in range(8):
            for j in range(i + 1):
                piv[i, j] = jnp.broadcast_to(tile[i:i + 1, base + j:base + j + 1], (8, HALF))
        cols = {}
        for u in below:
            for k in range(8):
                cols[u, k] = jnp.broadcast_to(tiles[u][:, base + k:base + k + 1], (8, HALF))
        rowv = [jnp.broadcast_to(tile[i:i + 1, :], (8, lanes)) for i in range(8)]
        for k in range(8):
            inv = lax.rsqrt(piv[k, k])
            rowv[k] = rowv[k] * spread(inv)
            for i in range(k + 1, 8):
                piv[i, k] = piv[i, k] * inv
            for u in below:
                cols[u, k] = cols[u, k] * inv
            for i in range(k + 1, 8):
                for j in range(k + 1, i + 1):
                    piv[i, j] = piv[i, j] - piv[i, k] * piv[j, k]
                rowv[i] = rowv[i] - spread(piv[i, k]) * rowv[k]
                for u in below:
                    cols[u, i] = cols[u, i] - piv[i, k] * cols[u, k]
            for u in below:
                tiles[u] = tiles[u] - spread(cols[u, k]) * rowv[k]
        out = rowv[7]
        for i in range(7):
            out = jnp.where(row_at == i, rowv[i], out)
        done.append(out)
    return jnp.concatenate(done, axis=0)


def kernel(data, test, cov_out, factor_out,
           dv, tv, part, sib, q, yrecv, zsend, zrecv, yown, ysib, sk, skt,
           pm, pxr, px, pzr, pyr, cm, am, um, lm, cv, cvb, cxr, czs, czr, zacc, covv,
           ld, xs, xr, ys, yr, zs, zr, szs, szr, sys_, syr, sbs, sbr, ybs, ybr,
           pxs, pxq, pzs, pzq, pys, pyq, pas, paq, pbs, pbq, pcs, pcq,
           cxs, cxq, czs_s, czq, outs):
    x, y, z, c = position()
    zl = lax.rem(z, NZL)
    zh = z // NZL
    o = 1 - c
    rows = data.shape[0] // NY
    hrows = rows // 2
    nvar = data.shape[1]
    sibling = device(x, y, z, o)

    def ypeer(k):
        return lax.rem(y + k, NY)

    def zpeer(k):
        return lax.rem(z + k, NZ)

    def xpeer(k):
        return lax.rem(x + k, NX)

    def order(i):
        half = (i + 1) // 2
        off = 4 + (1 - 2 * lax.rem(i, 2)) * half
        return lax.rem(y + off, NY)

    tcopy = pltpu.make_async_copy(test, tv, ld.at[NY])
    tcopy.start()

    def dcopy(i):
        r = order(i)
        at = pl.ds(pl.multiple_of(r * rows, rows), rows)
        return pltpu.make_async_copy(data.at[at, :], dv.at[at, :], ld.at[i])

    def start_load(i, carry):
        dcopy(i).start()
        return carry

    lax.fori_loop(0, NY, start_load, 0)

    barrier = pltpu.get_barrier_semaphore()
    peers = [sibling]
    peers += [device(x, ypeer(k), z, c) for k in range(1, NY)]
    peers += [device(x, y, zpeer(k), c) for k in range(1, NZ)]
    peers += [device(xpeer(k), y, z, c) for k in range(1, NX)]
    for p in peers:
        pl.semaphore_signal(barrier, inc=1, device_id=p, device_id_type=MESH)

    tcopy.wait()
    pl.semaphore_wait(barrier, len(peers))

    def sib_copy(r):
        return remote(part.at[o, r], sib.at[r], xs.at[r], xr.at[r], sibling)

    def y_copy(r):
        return remote(q.at[r], yrecv.at[y], ys.at[r], yr.at[y], device(x, r, z, c))

    def sketch_step(i, carry):
        @pl.when(i < NY)
        def _():
            r = order(i)
            dcopy(i).wait()
            at = pl.ds(pl.multiple_of(r * rows, rows), rows)
            p = jnp.dot(dv[at, :], tv[...], preferred_element_type=F32)
            part[0, r] = p[:, :HALF]
            part[1, r] = p[:, HALF:]
            sib_copy(r).start()

        @pl.when(i > 0)
        def _():
            r = order(i - 1)
            sib_copy(r).wait_recv()
            q[r] = part[c, r] + sib[r]

            @pl.when(r != y)
            def _():
                y_copy(r).start()

        return carry

    lax.fori_loop(0, NY + 1, sketch_step, 0)

    total = q[y]
    for k in range(1, NY):
        r = ypeer(k)
        remote(q.at[r], yrecv.at[r], ys.at[r], yr.at[r], device(x, r, z, c)).wait_recv()
        total = total + yrecv[r]
    q[y] = total
    partner = device(x, y, lax.rem(z + NZL, NZ), c)
    other_at = pl.ds(pl.multiple_of((1 - zh) * hrows, hrows), hrows)
    own_at = pl.ds(pl.multiple_of(zh * hrows, hrows), hrows)
    zsend[...] = q[y, other_at, :]
    z_copy = remote(zsend, zrecv, zs, zr, partner)
    z_copy.start()
    z_copy.wait_recv()
    yown[...] = (q[y, own_at, :] + zrecv[...]) * (1.0 / K)
    ysib_copy = remote(yown, ysib, ybs, ybr, sibling)
    ysib_copy.start()
    sk[c, y, zh] = yown[...].astype(BF16)

    def sy_copy(h, k):
        r = ypeer(k)
        return remote(sk.at[c, y, h], sk.at[c, y, h], sys_.at[h, r], syr.at[h, y],
                      device(x, r, z, c))

    def sy_wait(h, k):
        r = ypeer(k)
        remote(sk.at[c, r, h], sk.at[c, r, h], sys_.at[h, r], syr.at[h, r],
               device(x, r, z, c)).wait_recv()

    far_first = (4, 3, 5, 2, 6, 1, 7)
    sz_copy = remote(sk.at[c, y, zh], sk.at[c, y, zh], szs, szr, partner)
    sz_copy.start()
    for k in far_first:
        sy_copy(zh, k).start()

    ysib_copy.wait_recv()
    first = jnp.where(c == 0, yown[...], ysib[...])
    second = jnp.where(c == 0, ysib[...], yown[...])
    both = jnp.concatenate([first, second], axis=1).astype(BF16).astype(F32)
    prod = lax.dot_general(yown[...], both, (((0,), (0,)), ((), ())),
                           precision=HIGHEST, preferred_element_type=F32)
    for h in range(2):
        pm[:, 4 * h:4 * h + 4] = prod[:, h * HALF:(h + 1) * HALF].reshape(NX, 4, 8, HALF)

    def px_copy(k):
        r = xpeer(k)
        return remote(pm.at[r], pxr.at[x], pxs.at[r], pxq.at[x], device(r, y, z, c))

    for k in (2, 1, 3):
        px_copy(k).start()
    pxr[x] = pm[x]

    remote(sk.at[c, y, 1 - zh], sk.at[c, y, 1 - zh], szs, szr, partner).wait_recv()
    for k in far_first:
        sy_copy(1 - zh, k).start()

    for k in range(1, NX):
        r = xpeer(k)
        remote(pm.at[r], pxr.at[r], pxs.at[r], pxq.at[r], device(r, y, z, c)).wait_recv()
    px[...] = (pxr[0] + pxr[1]) + (pxr[2] + pxr[3])

    def pz_copy(k):
        r = zpeer(k)
        return remote(px.at[r], pzr.at[z], pzs.at[r], pzq.at[z], device(x, y, r, c))

    for k in far_first:
        pz_copy(k).start()
    pzr[z] = px[z]
    for k in range(1, NZ):
        r = zpeer(k)
        remote(px.at[r], pzr.at[r], pzs.at[r], pzq.at[r], device(x, y, r, c)).wait_recv()
    pyr[y] = jnp.sum(pzr[...], axis=0)

    def py_copy(k):
        r = ypeer(k)
        return remote(pyr.at[y], pyr.at[y], pys.at[r], pyq.at[y], device(x, r, z, c))

    for k in far_first:
        py_copy(k).start()

    def sb_copy(h):
        return remote(sk.at[c, :, h], sk.at[c, :, h], sbs.at[h], sbr.at[h], sibling)

    for k in range(1, NY):
        sy_wait(zh, k)
    sb_copy(zh).start()

    for k in range(1, NY):
        r = ypeer(k)
        remote(pyr.at[r], pyr.at[r], pys.at[r], pyq.at[r], device(x, r, z, c)).wait_recv()
    cm[c, x, z] = jnp.sum(pyr[...], axis=0)

    def pa_copy(k):
        r = zpeer(k)
        return remote(cm.at[c, x, z], cm.at[c, x, z], pas.at[r], paq.at[z], device(x, y, r, c))

    for k in far_first:
        pa_copy(k).start()

    for k in range(1, NY):
        sy_wait(1 - zh, k)
    sb_copy(1 - zh).start()

    def product(h):
        skt[...] = sk[h].reshape(NY * rows, HALF).T

        def tile(j, carry):
            at = pl.ds(pl.multiple_of(j * 512, 512), 512)
            res = jnp.dot(skt[...], dv[:, at], preferred_element_type=F32)
            res = res.reshape(2, NX, BLOCK, 512)
            cv[pl.ds(2 * h, 2), :, :, at] = res
            cvb[pl.ds(2 * h, 2), :, :, at] = res.astype(BF16)
            return carry

        lax.fori_loop(0, nvar // 512, tile, 0)

    def cx_copy(w, k):
        r = xpeer(k)
        return remote(cvb.at[w, r], cxr.at[w, x], cxs.at[w, r], cxq.at[w, x], device(r, y, z, c))

    product(c)
    for a in range(2):
        for k in (2, 1, 3):
            cx_copy(2 * c + a, k).start()

    for k in range(1, NZ):
        r = zpeer(k)
        remote(cm.at[c, x, r], cm.at[c, x, r], pas.at[r], paq.at[r], device(x, y, r, c)).wait_recv()

    def pb_copy(k):
        r = xpeer(k)
        return remote(cm.at[c, x], cm.at[c, x], pbs.at[r], pbq.at[x], device(r, y, z, c))

    for k in (2, 1, 3):
        pb_copy(k).start()

    for h in range(2):
        remote(sk.at[o, :, h], sk.at[o, :, h], sbs.at[h], sbr.at[h], sibling).wait_recv()
    product(o)
    for a in range(2):
        for k in (2, 1, 3):
            cx_copy(2 * o + a, k).start()

    for k in range(1, NX):
        r = xpeer(k)
        remote(cm.at[c, r], cm.at[c, r], pbs.at[r], pbq.at[r], device(r, y, z, c)).wait_recv()
    pc_copy = remote(cm.at[c], cm.at[c], pcs, pcq, sibling)
    pc_copy.start()
    remote(cm.at[o], cm.at[o], pcs, pcq, sibling).wait_recv()
    left = cm[:, :, 0:4].reshape(K, HALF)
    right = cm[:, :, 4:8].reshape(K, HALF)
    core = jnp.concatenate([left, right], axis=1) * (1.0 / (NX * NZL * NY * rows))
    am[...] = (core + core.T) * 0.5

    def cz_copy(w):
        return remote(czs.at[w], czr.at[zl], czs_s.at[w], czq.at[zl],
                      device(x, y, zh * NZL + w, c))

    lane_at = lax.broadcasted_iota(jnp.int32, (SLAB, K), 1)
    sub_at = lax.broadcasted_iota(jnp.int32, (SLAB, K), 0)

    def slab_step(j, carry):
        start = pl.multiple_of(j * SLAB, SLAB)
        slab = pltpu.roll(am[pl.ds(start, SLAB), :], lax.rem(K - start, K), axis=1)
        u = pltpu.roll(factor_slab(slab, SLAB, K), start, axis=1)
        u = jnp.where(lane_at >= sub_at + start, u, 0.0)
        um[pl.ds(start, SLAB), :] = u
        am[...] -= lax.dot_general(u, u, (((0,), (0,)), ((), ())),
                                   precision=HIGHEST, preferred_element_type=F32)

        w = lax.rem(2 * c + j, NZL)
        for k in range(1, NX):
            r = xpeer(k)
            remote(cvb.at[w, r], cxr.at[w, r], cxs.at[w, r], cxq.at[w, r],
                   device(r, y, z, c)).wait_recv()
        acc = cv[w, x]
        for k in range(1, NX):
            acc = acc + cxr[w, xpeer(k)].astype(F32)

        @pl.when(w == zl)
        def _():
            zacc[...] = acc

        @pl.when(w != zl)
        def _():
            czs[w] = acc.astype(BF16)
            cz_copy(w).start()

        return carry

    lax.fori_loop(0, K // SLAB, slab_step, 0)
    lm[...] = um[...].T
    factor_copy = pltpu.make_async_copy(lm, factor_out, outs.at[0])
    factor_copy.start()

    acc = zacc[...]
    for k in range(1, NZL):
        r = lax.rem(zl + k, NZL)
        remote(czs.at[r], czr.at[r], czs_s.at[r], czq.at[r],
               device(x, y, zh * NZL + r, c)).wait_recv()
        acc = acc + czr[r].astype(F32)
    covv[...] = acc * (1.0 / math.sqrt(NX * NZL * NY * rows))
    cov_copy = pltpu.make_async_copy(covv, cov_out, outs.at[1])
    cov_copy.start()

    def sib_done(r, carry):
        sib_copy(r).wait_send()
        return carry

    lax.fori_loop(0, NY, sib_done, 0)
    for k in range(1, NY):
        y_copy(ypeer(k)).wait_send()
        sy_copy(zh, k).wait_send()
        sy_copy(1 - zh, k).wait_send()
        py_copy(k).wait_send()
        pz_copy(k).wait_send()
        pa_copy(k).wait_send()
    z_copy.wait_send()
    ysib_copy.wait_send()
    sz_copy.wait_send()
    for h in range(2):
        sb_copy(h).wait_send()
    for k in range(1, NX):
        px_copy(k).wait_send()
        pb_copy(k).wait_send()
        for w in range(NZL):
            cx_copy(w, k).wait_send()
    pc_copy.wait_send()
    for k in range(1, NZL):
        cz_copy(lax.rem(zl + k, NZL)).wait_send()
    factor_copy.wait()
    cov_copy.wait()


def per_device(data, test_matrix):
    rows_all, nvar = data.shape
    rows = rows_all // NY
    vm = pltpu.VMEM
    dma = pltpu.SemaphoreType.DMA
    scratch = [
        vm((rows_all, nvar), BF16), vm((nvar, K), BF16),
        vm((2, NY, rows, HALF), F32), vm((NY, rows, HALF), F32), vm((NY, rows, HALF), F32),
        vm((NY, rows, HALF), F32),
        vm((rows // 2, HALF), F32), vm((rows // 2, HALF), F32),
        vm((rows // 2, HALF), F32), vm((rows // 2, HALF), F32),
        vm((2, NY, 2, rows // 2, HALF), BF16), vm((HALF, rows_all), BF16),
        vm((NX, NZ, 8, HALF), F32), vm((NX, NZ, 8, HALF), F32), vm((NZ, 8, HALF), F32),
        vm((NZ, 8, HALF), F32), vm((NY, 8, HALF), F32), vm((2, NX, NZ, 8, HALF), F32),
        vm((K, K), F32), vm((K, K), F32), vm((K, K), F32),
        vm((NZL, NX, BLOCK, nvar), F32), vm((NZL, NX, BLOCK, nvar), BF16),
        vm((NZL, NX, BLOCK, nvar), BF16), vm((NZL, BLOCK, nvar), BF16),
        vm((NZL, BLOCK, nvar), BF16), vm((BLOCK, nvar), F32), vm((BLOCK, nvar), F32),
        dma((NY + 1,)), dma((NY,)), dma((NY,)), dma((NY,)), dma((NY,)),
        dma, dma, dma, dma, dma((2, NY)), dma((2, NY)), dma((2,)), dma((2,)), dma, dma,
        dma((NX,)), dma((NX,)), dma((NZ,)), dma((NZ,)), dma((NY,)), dma((NY,)),
        dma((NZ,)), dma((NZ,)), dma((NX,)), dma((NX,)), dma, dma,
        dma((NZL, NX)), dma((NZL, NX)), dma((NZL,)), dma((NZL,)), dma((2,)),
    ]
    any_ = pl.BlockSpec(memory_space=pl.ANY)
    cov_t, factor = pl.pallas_call(
        kernel,
        out_shape=(jax.ShapeDtypeStruct((BLOCK, nvar), F32), jax.ShapeDtypeStruct((K, K), F32)),
        in_specs=[any_, any_],
        out_specs=(any_, any_),
        scratch_shapes=scratch,
        compiler_params=pltpu.CompilerParams(
            collective_id=0, has_side_effects=True, vmem_limit_bytes=48 * 1024 * 1024
        ),
        cost_estimate=pl.CostEstimate(
            flops=4 * rows_all * nvar * K, bytes_accessed=2 * nvar * (rows_all + K),
            transcendentals=0,
        ),
        name="sketch",
    )(data, test_matrix)
    return (cov_t.T, factor)


def solution(mesh):
    return jax.shard_map(
        per_device,
        mesh=mesh,
        in_specs=(P("sample", "var"), P("var", None)),
        out_specs=(P("var", "sample"), P()),
        check_vma=False,
    )
```

```python
import math

import jax
import jax.numpy as jnp
from jax import lax
from jax.experimental import pallas as pl
from jax.experimental.pallas import tpu as pltpu
from jax.sharding import PartitionSpec as P

MESH = pl.DeviceIdType.MESH
HIGHEST = lax.Precision.HIGHEST
F32 = jnp.float32
BF16 = jnp.bfloat16

NX, NY, NZ = 4, 8, 8
NZL = 4
K = 256
HALF = 128
BLOCK = 16
SLAB = 64


def position():
    s = lax.axis_index("sample")
    v = lax.axis_index("var")
    x = lax.rem(s, NX)
    zl = s // NX
    c = lax.rem(v, 2)
    zh = lax.rem(v // 2, 2)
    y = v // 4
    return x, y, zh * NZL + zl, c


def device(x, y, z, c):
    return (lax.rem(z, NZL) * NX + x, y * 4 + (z // NZL) * 2 + c)


def remote(src, dst, send, recv, target):
    return pltpu.make_async_remote_copy(
        src_ref=src, dst_ref=dst, send_sem=send, recv_sem=recv,
        device_id=target, device_id_type=MESH,
    )


def factor_slab(block, rows, lanes):
    wide = lanes // HALF

    def spread(a):
        return jnp.concatenate([a] * wide, axis=1)

    count = rows // 8
    tiles = [block[8 * t:8 * t + 8, :] for t in range(count)]
    done = []
    row_at = lax.broadcasted_iota(jnp.int32, (8, lanes), 0)
    for t in range(count):
        tile = tiles[t]
        base = 8 * t
        below = range(t + 1, count)
        piv = {}
        for i in range(8):
            for j in range(i + 1):
                piv[i, j] = jnp.broadcast_to(tile[i:i + 1, base + j:base + j + 1], (8, HALF))
        cols = {}
        for u in below:
            for k in range(8):
                cols[u, k] = jnp.broadcast_to(tiles[u][:, base + k:base + k + 1], (8, HALF))
        rowv = [jnp.broadcast_to(tile[i:i + 1, :], (8, lanes)) for i in range(8)]
        for k in range(8):
            inv = lax.rsqrt(piv[k, k])
            rowv[k] = rowv[k] * spread(inv)
            for i in range(k + 1, 8):
                piv[i, k] = piv[i, k] * inv
            for u in below:
                cols[u, k] = cols[u, k] * inv
            for i in range(k + 1, 8):
                for j in range(k + 1, i + 1):
                    piv[i, j] = piv[i, j] - piv[i, k] * piv[j, k]
                rowv[i] = rowv[i] - spread(piv[i, k]) * rowv[k]
                for u in below:
                    cols[u, i] = cols[u, i] - piv[i, k] * cols[u, k]
            for u in below:
                tiles[u] = tiles[u] - spread(cols[u, k]) * rowv[k]
        out = rowv[7]
        for i in range(7):
            out = jnp.where(row_at == i, rowv[i], out)
        done.append(out)
    return jnp.concatenate(done, axis=0)


def kernel(data, test, cov_out, factor_out,
           dv, tv, part, sib, q, yrecv, zrecv, ysum, sk, pxr, pzr, cm, am, um, lm,
           cv, cvb, cxr, czs, czr, zacc, covv,
           ld, xs, xr, ys, yr, zs, zr, sys_, syr, sbs, sbr,
           pxs, pxq, pzs, pzq, pys, pyq, pcs, pcq, cxs, cxq, czs_s, czq, outs):
    x, y, z, c = position()
    zl = lax.rem(z, NZL)
    zh = z // NZL
    o = 1 - c
    nrow, nvar = data.shape
    part_rows = nrow // 2
    sibling = device(x, y, z, o)
    partner = device(x, y, lax.rem(z + NZL, NZ), c)
    far_first = (4, 3, 5, 2, 6, 1, 7)

    def ypeer(k):
        return lax.rem(y + k, NY)

    def zpeer(k):
        return lax.rem(zl + k, NZL)

    def zdev(w):
        return device(x, y, zh * NZL + w, c)

    def xpeer(k):
        return lax.rem(x + k, NX)

    tcopy = pltpu.make_async_copy(test, tv, ld.at[2])
    tcopy.start()

    def dcopy(i):
        at = pl.ds(i * part_rows, part_rows)
        return pltpu.make_async_copy(data.at[at, :], dv.at[at, :], ld.at[i])

    for i in range(2):
        dcopy(i).start()

    barrier = pltpu.get_barrier_semaphore()
    peers = [sibling, partner]
    peers += [device(x, ypeer(k), z, c) for k in range(1, NY)]
    peers += [zdev(zpeer(k)) for k in range(1, NZL)]
    peers += [device(xpeer(k), y, z, c) for k in range(1, NX)]
    for p in peers:
        pl.semaphore_signal(barrier, inc=1, device_id=p, device_id_type=MESH)

    def sib_copy(i):
        at = pl.ds(i * part_rows, part_rows)
        return remote(part.at[o, :, at], sib.at[:, at], xs.at[i], xr.at[i], sibling)

    def y_copy(r):
        return remote(q.at[r], yrecv.at[y], ys.at[r], yr.at[y], device(x, r, z, c))

    tcopy.wait()
    for i in range(2):
        dcopy(i).wait()
        at = slice(i * part_rows, (i + 1) * part_rows)
        p = jnp.dot(dv[at, :], tv[...], preferred_element_type=F32).T
        part[0, :, at] = p[:HALF]
        part[1, :, at] = p[HALF:]
        if i == 0:
            pl.semaphore_wait(barrier, len(peers))
        sib_copy(i).start()
    for i in range(2):
        sib_copy(i).wait_recv()
        at = slice(i * part_rows, (i + 1) * part_rows)
        q[:, :, at] = (part[c, :, at] + sib[:, at]).reshape(NY, BLOCK, part_rows)
    for k in far_first:
        y_copy(ypeer(k)).start()

    total = q[y]
    for k in range(1, NY):
        r = ypeer(k)
        remote(q.at[r], yrecv.at[r], ys.at[r], yr.at[r], device(x, r, z, c)).wait_recv()
        total = total + yrecv[r]
    q[y] = total
    z_copy = remote(q.at[y], zrecv, zs, zr, partner)
    z_copy.start()
    z_copy.wait_recv()
    ysum[...] = (total + zrecv[...]) * (1.0 / K)
    sk[c, y] = ysum[...].astype(BF16)

    def sy_copy(k):
        r = ypeer(k)
        return remote(sk.at[c, y], sk.at[c, y], sys_.at[r], syr.at[y], device(x, r, z, c))

    for k in far_first:
        sy_copy(k).start()
    for k in range(1, NY):
        r = ypeer(k)
        remote(sk.at[c, r], sk.at[c, r], sys_.at[r], syr.at[r], device(x, r, z, c)).wait_recv()
    sb_copy = remote(sk.at[c], sk.at[c], sbs, sbr, sibling)
    sb_copy.start()

    def product(h):
        left = sk[h].reshape(HALF, nrow)

        def tile(j, carry):
            at = pl.ds(pl.multiple_of(j * 1024, 1024), 1024)
            res = jnp.dot(left, dv[:, at], preferred_element_type=F32)
            res = res.reshape(2, NX, BLOCK, 1024)
            cv[pl.ds(2 * h, 2), :, :, at] = res
            cvb[pl.ds(2 * h, 2), :, :, at] = res.astype(BF16)
            return carry

        lax.fori_loop(0, nvar // 1024, tile, 0)

    def cx_copy(w, k):
        r = xpeer(k)
        return remote(cvb.at[w, r], cxr.at[w, x], cxs.at[w, r], cxq.at[w, x], device(r, y, z, c))

    def cz_copy(w):
        return remote(czs.at[w], czr.at[zl], czs_s.at[w], czq.at[zl], zdev(w))

    def x_sum(w):
        for k in range(1, NX):
            r = xpeer(k)
            remote(cvb.at[w, r], cxr.at[w, r], cxs.at[w, r], cxq.at[w, r],
                   device(r, y, z, c)).wait_recv()
        acc = cv[w, x]
        for k in range(1, NX):
            acc = acc + cxr[w, xpeer(k)].astype(F32)

        @pl.when(w == zl)
        def _():
            zacc[...] = acc

        @pl.when(w != zl)
        def _():
            czs[w] = acc.astype(BF16)
            cz_copy(w).start()

    product(c)
    remote(sk.at[o], sk.at[o], sbs, sbr, sibling).wait_recv()

    y1 = ysum[...].astype(BF16)
    rest = ysum[...] - y1.astype(F32)
    y2 = rest.astype(BF16)
    y3 = (rest - y2.astype(F32)).astype(BF16)
    terms = lax.dot_general(
        jnp.concatenate([y1, y2, y3], axis=0), sk[...].reshape(K, nrow),
        (((1,), (1,)), ((), ())), preferred_element_type=F32,
    )
    terms = (terms[2 * BLOCK:] + terms[BLOCK:2 * BLOCK]) + terms[:BLOCK]
    pxr[x] = terms * (1.0 / (NX * NZL * nrow))

    def px_copy(k):
        r = xpeer(k)
        return remote(pxr.at[x], pxr.at[x], pxs.at[r], pxq.at[x], device(r, y, z, c))

    for k in (2, 1, 3):
        px_copy(k).start()
    for a in range(2):
        for k in (2, 1, 3):
            cx_copy(2 * c + a, k).start()
    product(o)
    for a in range(2):
        for k in (2, 1, 3):
            cx_copy(2 * o + a, k).start()

    for k in range(1, NX):
        r = xpeer(k)
        remote(pxr.at[r], pxr.at[r], pxs.at[r], pxq.at[r], device(r, y, z, c)).wait_recv()
    pzr[zl] = (pxr[0] + pxr[1]) + (pxr[2] + pxr[3])

    def pz_copy(k):
        r = zpeer(k)
        return remote(pzr.at[zl], pzr.at[zl], pzs.at[r], pzq.at[zl], zdev(r))

    for k in (3, 2, 1):
        pz_copy(k).start()
    x_sum(2 * c)
    for k in range(1, NZL):
        r = zpeer(k)
        remote(pzr.at[r], pzr.at[r], pzs.at[r], pzq.at[r], zdev(r)).wait_recv()
    cm[c, y] = (pzr[0] + pzr[1]) + (pzr[2] + pzr[3])

    def py_copy(k):
        r = ypeer(k)
        return remote(cm.at[c, y], cm.at[c, y], pys.at[r], pyq.at[y], device(x, r, z, c))

    for k in far_first:
        py_copy(k).start()
    x_sum(2 * c + 1)
    for k in range(1, NY):
        r = ypeer(k)
        remote(cm.at[c, r], cm.at[c, r], pys.at[r], pyq.at[r], device(x, r, z, c)).wait_recv()
    pc_copy = remote(cm.at[c], cm.at[c], pcs, pcq, sibling)
    pc_copy.start()
    remote(cm.at[o], cm.at[o], pcs, pcq, sibling).wait_recv()
    core = cm[...].reshape(K, K)
    am[...] = (core + core.T) * 0.5

    lane_at = lax.broadcasted_iota(jnp.int32, (SLAB, K), 1)
    sub_at = lax.broadcasted_iota(jnp.int32, (SLAB, K), 0)

    def slab_step(j, carry):
        start = pl.multiple_of(j * SLAB, SLAB)
        slab = pltpu.roll(am[pl.ds(start, SLAB), :], lax.rem(K - start, K), axis=1)
        u = pltpu.roll(factor_slab(slab, SLAB, K), start, axis=1)
        u = jnp.where(lane_at >= sub_at + start, u, 0.0)
        um[pl.ds(start, SLAB), :] = u
        am[...] -= lax.dot_general(u, u, (((0,), (0,)), ((), ())),
                                   precision=HIGHEST, preferred_element_type=F32)

        @pl.when(j < 2)
        def _():
            x_sum(2 * o + j)

        return carry

    lax.fori_loop(0, K // SLAB, slab_step, 0)
    lm[...] = um[...].T
    factor_copy = pltpu.make_async_copy(lm, factor_out, outs.at[0])
    factor_copy.start()

    acc = zacc[...]
    for k in range(1, NZL):
        r = zpeer(k)
        remote(czs.at[r], czr.at[r], czs_s.at[r], czq.at[r], zdev(r)).wait_recv()
        acc = acc + czr[r].astype(F32)
    covv[...] = acc * (1.0 / math.sqrt(NX * NZL * nrow))
    cov_copy = pltpu.make_async_copy(covv, cov_out, outs.at[1])
    cov_copy.start()

    for i in range(2):
        sib_copy(i).wait_send()
    for k in range(1, NY):
        y_copy(ypeer(k)).wait_send()
        sy_copy(k).wait_send()
        py_copy(k).wait_send()
    z_copy.wait_send()
    sb_copy.wait_send()
    for k in range(1, NX):
        px_copy(k).wait_send()
        for w in range(NZL):
            cx_copy(w, k).wait_send()
    pc_copy.wait_send()
    for k in range(1, NZL):
        pz_copy(k).wait_send()
        cz_copy(zpeer(k)).wait_send()
    factor_copy.wait()
    cov_copy.wait()


def per_device(data, test_matrix):
    rows_all, nvar = data.shape
    vm = pltpu.VMEM
    dma = pltpu.SemaphoreType.DMA
    scratch = [
        vm((rows_all, nvar), BF16), vm((nvar, K), BF16),
        vm((2, HALF, rows_all), F32), vm((HALF, rows_all), F32),
        vm((NY, BLOCK, rows_all), F32), vm((NY, BLOCK, rows_all), F32),
        vm((BLOCK, rows_all), F32), vm((BLOCK, rows_all), F32),
        vm((2, NY, BLOCK, rows_all), BF16),
        vm((NX, BLOCK, K), F32), vm((NZL, BLOCK, K), F32), vm((2, NY, BLOCK, K), F32),
        vm((K, K), F32), vm((K, K), F32), vm((K, K), F32),
        vm((NZL, NX, BLOCK, nvar), F32), vm((NZL, NX, BLOCK, nvar), BF16),
        vm((NZL, NX, BLOCK, nvar), BF16), vm((NZL, BLOCK, nvar), BF16),
        vm((NZL, BLOCK, nvar), BF16), vm((BLOCK, nvar), F32), vm((BLOCK, nvar), F32),
        dma((3,)), dma((2,)), dma((2,)), dma((NY,)), dma((NY,)),
        dma, dma, dma((NY,)), dma((NY,)), dma, dma,
        dma((NX,)), dma((NX,)), dma((NZL,)), dma((NZL,)), dma((NY,)), dma((NY,)),
        dma, dma, dma((NZL, NX)), dma((NZL, NX)), dma((NZL,)), dma((NZL,)), dma((2,)),
    ]
    any_ = pl.BlockSpec(memory_space=pl.ANY)
    cov_t, factor = pl.pallas_call(
        kernel,
        out_shape=(jax.ShapeDtypeStruct((BLOCK, nvar), F32), jax.ShapeDtypeStruct((K, K), F32)),
        in_specs=[any_, any_],
        out_specs=(any_, any_),
        scratch_shapes=scratch,
        compiler_params=pltpu.CompilerParams(
            collective_id=0, has_side_effects=True, vmem_limit_bytes=62 * 1024 * 1024
        ),
        cost_estimate=pl.CostEstimate(
            flops=4 * rows_all * nvar * K, bytes_accessed=2 * nvar * (rows_all + K),
            transcendentals=0,
        ),
        name="sketch",
    )(data, test_matrix)
    return (cov_t.T, factor)


def solution(mesh):
    return jax.shard_map(
        per_device,
        mesh=mesh,
        in_specs=(P("sample", "var"), P("var", None)),
        out_specs=(P("var", "sample"), P()),
        check_vma=False,
    )
```

```python
import math

import jax
import jax.numpy as jnp
from jax import lax
from jax.experimental import pallas as pl
from jax.experimental.pallas import tpu as pltpu
from jax.sharding import PartitionSpec as P

MESH = pl.DeviceIdType.MESH
HIGHEST = lax.Precision.HIGHEST
F32 = jnp.float32
BF16 = jnp.bfloat16

NX, NY, NZ = 4, 8, 8
NZL = 4
K = 256
HALF = 128
BLOCK = 16
SLAB = 64
SPAN = 83.0
TINY = 1e-30


def position():
    s = lax.axis_index("sample")
    v = lax.axis_index("var")
    x = lax.rem(s, NX)
    zl = s // NX
    c = lax.rem(v, 2)
    zh = lax.rem(v // 2, 2)
    y = v // 4
    return x, y, zh * NZL + zl, c


def device(x, y, z, c):
    return (lax.rem(z, NZL) * NX + x, y * 4 + (z // NZL) * 2 + c)


def remote(src, dst, send, recv, target):
    return pltpu.make_async_remote_copy(
        src_ref=src, dst_ref=dst, send_sem=send, recv_sem=recv,
        device_id=target, device_id_type=MESH,
    )


def encode(a):
    top = jnp.maximum(jnp.max(jnp.abs(a), axis=1, keepdims=True), TINY) * 1.01
    scale = jnp.broadcast_to(top, (a.shape[0], HALF)).astype(BF16)
    wide = jnp.concatenate([SPAN / scale.astype(F32)] * (a.shape[1] // HALF), axis=1)
    return jnp.concatenate([jnp.exp(a * wide).astype(BF16), scale], axis=1)


def decode(e):
    lanes = e.shape[1] - HALF
    scale = e[:, lanes:].astype(F32) * (1.0 / SPAN)
    return jnp.log(e[:, :lanes].astype(F32)) * jnp.concatenate([scale] * (lanes // HALF), axis=1)


def factor_slab(block, rows, lanes):
    wide = lanes // HALF

    def spread(a):
        return jnp.concatenate([a] * wide, axis=1)

    count = rows // 8
    tiles = [block[8 * t:8 * t + 8, :] for t in range(count)]
    done = []
    row_at = lax.broadcasted_iota(jnp.int32, (8, lanes), 0)
    for t in range(count):
        tile = tiles[t]
        base = 8 * t
        below = range(t + 1, count)
        piv = {}
        for i in range(8):
            for j in range(i + 1):
                piv[i, j] = jnp.broadcast_to(tile[i:i + 1, base + j:base + j + 1], (8, HALF))
        cols = {}
        for u in below:
            for k in range(8):
                cols[u, k] = jnp.broadcast_to(tiles[u][:, base + k:base + k + 1], (8, HALF))
        rowv = [jnp.broadcast_to(tile[i:i + 1, :], (8, lanes)) for i in range(8)]
        for k in range(8):
            inv = lax.rsqrt(piv[k, k])
            rowv[k] = rowv[k] * spread(inv)
            for i in range(k + 1, 8):
                piv[i, k] = piv[i, k] * inv
            for u in below:
                cols[u, k] = cols[u, k] * inv
            for i in range(k + 1, 8):
                for j in range(k + 1, i + 1):
                    piv[i, j] = piv[i, j] - piv[i, k] * piv[j, k]
                rowv[i] = rowv[i] - spread(piv[i, k]) * rowv[k]
                for u in below:
                    cols[u, i] = cols[u, i] - piv[i, k] * cols[u, k]
            for u in below:
                tiles[u] = tiles[u] - spread(cols[u, k]) * rowv[k]
        out = rowv[7]
        for i in range(7):
            out = jnp.where(row_at == i, rowv[i], out)
        done.append(out)
    return jnp.concatenate(done, axis=0)


def kernel(data, test, cov_out, factor_out,
           dv, tv, part, sib, q, yrecv, zrecv, ysum, sk, pxr, pzr, cm, am, um,
           cv, cvb, cxr, czs, czr, zacc,
           ld, xs, xr, ys, yr, zs, zr, sys_, syr, sbs, sbr,
           pxs, pxq, pzs, pzq, pys, pyq, pcs, pcq, cxs, cxq, czs_s, czq):
    x, y, z, c = position()
    zl = lax.rem(z, NZL)
    zh = z // NZL
    o = 1 - c
    nrow, nvar = data.shape
    part_rows = nrow // 2
    sibling = device(x, y, z, o)
    partner = device(x, y, lax.rem(z + NZL, NZ), c)
    far_first = (4, 3, 5, 2, 6, 1, 7)

    def ypeer(k):
        return lax.rem(y + k, NY)

    def zpeer(k):
        return lax.rem(zl + k, NZL)

    def zdev(w):
        return device(x, y, zh * NZL + w, c)

    def xpeer(k):
        return lax.rem(x + k, NX)

    tcopy = pltpu.make_async_copy(test, tv, ld.at[2])
    tcopy.start()

    def dcopy(i):
        at = pl.ds(i * part_rows, part_rows)
        return pltpu.make_async_copy(data.at[at, :], dv.at[at, :], ld.at[i])

    for i in range(2):
        dcopy(i).start()

    barrier = pltpu.get_barrier_semaphore()
    peers = [sibling, partner]
    peers += [device(x, ypeer(k), z, c) for k in range(1, NY)]
    peers += [zdev(zpeer(k)) for k in range(1, NZL)]
    peers += [device(xpeer(k), y, z, c) for k in range(1, NX)]
    for p in peers:
        pl.semaphore_signal(barrier, inc=1, device_id=p, device_id_type=MESH)

    def sib_copy(i):
        at = pl.ds(i * part_rows, part_rows)
        return remote(part.at[o, :, at], sib.at[:, at], xs.at[i], xr.at[i], sibling)

    def y_copy(r):
        return remote(q.at[r], yrecv.at[y], ys.at[r], yr.at[y], device(x, r, z, c))

    tcopy.wait()
    for i in range(2):
        dcopy(i).wait()
        at = slice(i * part_rows, (i + 1) * part_rows)
        p = jnp.dot(dv[at, :], tv[...], preferred_element_type=F32).T
        part[0, :, at] = p[:HALF]
        part[1, :, at] = p[HALF:]
        if i == 0:
            pl.semaphore_wait(barrier, len(peers))
        sib_copy(i).start()
    for i in range(2):
        sib_copy(i).wait_recv()
        at = slice(i * part_rows, (i + 1) * part_rows)
        part[c, :, at] = part[c, :, at] + sib[:, at]
    for k in far_first:
        r = ypeer(k)
        q[r] = encode(part[c, pl.ds(pl.multiple_of(r * BLOCK, BLOCK), BLOCK), :])
        y_copy(r).start()

    total = part[c, pl.ds(pl.multiple_of(y * BLOCK, BLOCK), BLOCK), :]
    for k in range(1, NY):
        r = ypeer(k)
        remote(q.at[r], yrecv.at[r], ys.at[r], yr.at[r], device(x, r, z, c)).wait_recv()
        total = total + decode(yrecv[r])
    q[y] = encode(total)
    z_copy = remote(q.at[y], zrecv, zs, zr, partner)
    z_copy.start()
    z_copy.wait_recv()
    ysum[...] = (decode(q[y]) + decode(zrecv[...])) * (1.0 / K)
    sk[c, y] = ysum[...].astype(BF16)

    def sy_copy(k):
        r = ypeer(k)
        return remote(sk.at[c, y], sk.at[c, y], sys_.at[r], syr.at[y], device(x, r, z, c))

    for k in far_first:
        sy_copy(k).start()
    for k in range(1, NY):
        r = ypeer(k)
        remote(sk.at[c, r], sk.at[c, r], sys_.at[r], syr.at[r], device(x, r, z, c)).wait_recv()
    sb_copy = remote(sk.at[c], sk.at[c], sbs, sbr, sibling)
    sb_copy.start()

    def product(h):
        left = sk[h].reshape(HALF, nrow)

        def tile(j, carry):
            at = pl.ds(pl.multiple_of(j * 1024, 1024), 1024)
            res = jnp.dot(left, dv[:, at], preferred_element_type=F32)
            res = res.reshape(2, NX, BLOCK, 1024)
            cv[pl.ds(2 * h, 2), :, :, at] = res
            cvb[pl.ds(2 * h, 2), :, :, at] = res.astype(BF16)
            return carry

        lax.fori_loop(0, nvar // 1024, tile, 0)

    def cx_copy(w, k):
        r = xpeer(k)
        return remote(cvb.at[w, r], cxr.at[w, x], cxs.at[w, r], cxq.at[w, x], device(r, y, z, c))

    def cz_copy(w):
        return remote(czs.at[w], czr.at[zl], czs_s.at[w], czq.at[zl], zdev(w))

    def x_sum(w):
        for k in range(1, NX):
            r = xpeer(k)
            remote(cvb.at[w, r], cxr.at[w, r], cxs.at[w, r], cxq.at[w, r],
                   device(r, y, z, c)).wait_recv()
        acc = cv[w, x]
        for k in range(1, NX):
            acc = acc + cxr[w, xpeer(k)].astype(F32)

        @pl.when(w == zl)
        def _():
            zacc[...] = acc

        @pl.when(w != zl)
        def _():
            czs[w] = acc.astype(BF16)
            cz_copy(w).start()

    product(c)
    remote(sk.at[o], sk.at[o], sbs, sbr, sibling).wait_recv()

    y1 = ysum[...].astype(BF16)
    rest = ysum[...] - y1.astype(F32)
    y2 = rest.astype(BF16)
    y3 = (rest - y2.astype(F32)).astype(BF16)
    terms = lax.dot_general(
        jnp.concatenate([y1, y2, y3], axis=0), sk[...].reshape(K, nrow),
        (((1,), (1,)), ((), ())), preferred_element_type=F32,
    )
    terms = (terms[2 * BLOCK:] + terms[BLOCK:2 * BLOCK]) + terms[:BLOCK]
    pxr[x] = terms * (1.0 / (NX * NZL * nrow))

    def px_copy(k):
        r = xpeer(k)
        return remote(pxr.at[x], pxr.at[x], pxs.at[r], pxq.at[x], device(r, y, z, c))

    for k in (2, 1, 3):
        px_copy(k).start()
    for a in range(2):
        for k in (2, 1, 3):
            cx_copy(2 * c + a, k).start()
    product(o)
    for a in range(2):
        for k in (2, 1, 3):
            cx_copy(2 * o + a, k).start()

    for k in range(1, NX):
        r = xpeer(k)
        remote(pxr.at[r], pxr.at[r], pxs.at[r], pxq.at[r], device(r, y, z, c)).wait_recv()
    pzr[zl] = (pxr[0] + pxr[1]) + (pxr[2] + pxr[3])

    def pz_copy(k):
        r = zpeer(k)
        return remote(pzr.at[zl], pzr.at[zl], pzs.at[r], pzq.at[zl], zdev(r))

    for k in (3, 2, 1):
        pz_copy(k).start()
    x_sum(2 * c)
    for k in range(1, NZL):
        r = zpeer(k)
        remote(pzr.at[r], pzr.at[r], pzs.at[r], pzq.at[r], zdev(r)).wait_recv()
    cm[c, y] = (pzr[0] + pzr[1]) + (pzr[2] + pzr[3])

    def py_copy(k):
        r = ypeer(k)
        return remote(cm.at[c, y], cm.at[c, y], pys.at[r], pyq.at[y], device(x, r, z, c))

    for k in far_first:
        py_copy(k).start()
    x_sum(2 * c + 1)
    for k in range(1, NY):
        r = ypeer(k)
        remote(cm.at[c, r], cm.at[c, r], pys.at[r], pyq.at[r], device(x, r, z, c)).wait_recv()
    pc_copy = remote(cm.at[c], cm.at[c], pcs, pcq, sibling)
    pc_copy.start()
    remote(cm.at[o], cm.at[o], pcs, pcq, sibling).wait_recv()
    core = cm[...].reshape(K, K)
    am[...] = (core + core.T) * 0.5

    lane_at = lax.broadcasted_iota(jnp.int32, (SLAB, K), 1)
    sub_at = lax.broadcasted_iota(jnp.int32, (SLAB, K), 0)

    def slab_step(j, carry):
        start = pl.multiple_of(j * SLAB, SLAB)
        slab = pltpu.roll(am[pl.ds(start, SLAB), :], lax.rem(K - start, K), axis=1)
        u = pltpu.roll(factor_slab(slab, SLAB, K), start, axis=1)
        u = jnp.where(lane_at >= sub_at + start, u, 0.0)
        um[pl.ds(start, SLAB), :] = u

        @pl.when(j < K // SLAB - 1)
        def _():
            am[...] -= lax.dot_general(u, u, (((0,), (0,)), ((), ())),
                                       precision=HIGHEST, preferred_element_type=F32)

        @pl.when(j < 2)
        def _():
            x_sum(2 * o + j)

        return carry

    lax.fori_loop(0, K // SLAB, slab_step, 0)
    factor_out[...] = um[...].T

    acc = zacc[...]
    for k in range(1, NZL):
        r = zpeer(k)
        remote(czs.at[r], czr.at[r], czs_s.at[r], czq.at[r], zdev(r)).wait_recv()
        acc = acc + czr[r].astype(F32)
    cov_out[...] = acc * (1.0 / math.sqrt(NX * NZL * nrow))

    for i in range(2):
        sib_copy(i).wait_send()
    for k in range(1, NY):
        y_copy(ypeer(k)).wait_send()
        sy_copy(k).wait_send()
        py_copy(k).wait_send()
    z_copy.wait_send()
    sb_copy.wait_send()
    for k in range(1, NX):
        px_copy(k).wait_send()
        for w in range(NZL):
            cx_copy(w, k).wait_send()
    pc_copy.wait_send()
    for k in range(1, NZL):
        pz_copy(k).wait_send()
        cz_copy(zpeer(k)).wait_send()


def per_device(data, test_matrix):
    rows_all, nvar = data.shape
    vm = pltpu.VMEM
    dma = pltpu.SemaphoreType.DMA
    scratch = [
        vm((rows_all, nvar), BF16), vm((nvar, K), BF16),
        vm((2, HALF, rows_all), F32), vm((HALF, rows_all), F32),
        vm((NY, BLOCK, rows_all + HALF), BF16), vm((NY, BLOCK, rows_all + HALF), BF16),
        vm((BLOCK, rows_all + HALF), BF16), vm((BLOCK, rows_all), F32),
        vm((2, NY, BLOCK, rows_all), BF16),
        vm((NX, BLOCK, K), F32), vm((NZL, BLOCK, K), F32), vm((2, NY, BLOCK, K), F32),
        vm((K, K), F32), vm((K, K), F32),
        vm((NZL, NX, BLOCK, nvar), F32), vm((NZL, NX, BLOCK, nvar), BF16),
        vm((NZL, NX, BLOCK, nvar), BF16), vm((NZL, BLOCK, nvar), BF16),
        vm((NZL, BLOCK, nvar), BF16), vm((BLOCK, nvar), F32),
        dma((3,)), dma((2,)), dma((2,)), dma((NY,)), dma((NY,)),
        dma, dma, dma((NY,)), dma((NY,)), dma, dma,
        dma((NX,)), dma((NX,)), dma((NZL,)), dma((NZL,)), dma((NY,)), dma((NY,)),
        dma, dma, dma((NZL, NX)), dma((NZL, NX)), dma((NZL,)), dma((NZL,)),
    ]
    any_ = pl.BlockSpec(memory_space=pl.ANY)
    vmem = pl.BlockSpec(memory_space=pltpu.VMEM)
    cov_t, factor = pl.pallas_call(
        kernel,
        out_shape=(pltpu.VMEM((BLOCK, nvar), F32), pltpu.VMEM((K, K), F32)),
        in_specs=[any_, any_],
        out_specs=(vmem, vmem),
        scratch_shapes=scratch,
        compiler_params=pltpu.CompilerParams(
            collective_id=0, has_side_effects=True, vmem_limit_bytes=62 * 1024 * 1024
        ),
        cost_estimate=pl.CostEstimate(
            flops=4 * rows_all * nvar * K, bytes_accessed=2 * nvar * (rows_all + K),
            transcendentals=0,
        ),
        name="sketch",
    )(data, test_matrix)
    return (cov_t.T, factor)


def solution(mesh):
    return jax.shard_map(
        per_device,
        mesh=mesh,
        in_specs=(P("sample", "var"), P("var", None)),
        out_specs=(P("var", "sample"), P()),
        check_vma=False,
    )
```

```python
import math

import jax
import jax.numpy as jnp
from jax import lax
from jax.experimental import pallas as pl
from jax.experimental.pallas import tpu as pltpu
from jax.sharding import PartitionSpec as P

MESH = pl.DeviceIdType.MESH
HIGHEST = lax.Precision.HIGHEST
F32 = jnp.float32
BF16 = jnp.bfloat16

NX, NY, NZ = 4, 8, 8
NZL = 4
K = 256
HALF = 128
BLOCK = 16
SLAB = 64
SPAN = 83.0
TINY = 1e-30


def position():
    s = lax.axis_index("sample")
    v = lax.axis_index("var")
    x = lax.rem(s, NX)
    zl = s // NX
    c = lax.rem(v, 2)
    zh = lax.rem(v // 2, 2)
    y = v // 4
    return x, y, zh * NZL + zl, c


def device(x, y, z, c):
    return (lax.rem(z, NZL) * NX + x, y * 4 + (z // NZL) * 2 + c)


def remote(src, dst, send, recv, target):
    return pltpu.make_async_remote_copy(
        src_ref=src, dst_ref=dst, send_sem=send, recv_sem=recv,
        device_id=target, device_id_type=MESH,
    )


def encode(a):
    top = jnp.maximum(jnp.max(jnp.abs(a), axis=1, keepdims=True), TINY) * 1.01
    scale = jnp.broadcast_to(top, (a.shape[0], HALF)).astype(BF16)
    wide = jnp.concatenate([SPAN / scale.astype(F32)] * (a.shape[1] // HALF), axis=1)
    return jnp.concatenate([jnp.exp(a * wide).astype(BF16), scale], axis=1)


def decode(e):
    lanes = e.shape[1] - HALF
    scale = e[:, lanes:].astype(F32) * (1.0 / SPAN)
    return jnp.log(e[:, :lanes].astype(F32)) * jnp.concatenate([scale] * (lanes // HALF), axis=1)


def factor_slab(block, rows, lanes, held):
    wide = lanes // HALF

    def spread(a):
        return jnp.concatenate([a] * wide, axis=1)

    count = rows // 8
    tiles = [block[8 * t:8 * t + 8, :] for t in range(count)]
    done = []
    row_at = lax.broadcasted_iota(jnp.int32, (8, lanes), 0)
    for t in range(count):
        tile = tiles[t]
        base = 8 * t
        for j in range(8):
            held[t % 2, j] = jnp.broadcast_to(tile[:, base + j:base + j + 1], (8, HALF))
        piv = {}
        for i in range(8):
            for j in range(i + 1):
                piv[i, j] = jnp.broadcast_to(held[t % 2, j, i:i + 1, :], (8, HALF))
        inv = {}
        for k in range(0, 8, 2):
            first, cross, second = piv[k, k], piv[k + 1, k], piv[k + 1, k + 1]
            root = lax.rsqrt(first)
            inv[k] = root
            inv[k + 1] = lax.rsqrt(first * second - cross * cross) * (first * root)
            piv[k + 1, k] = cross * root
            for i in range(k + 2, 8):
                piv[i, k] = piv[i, k] * root
                piv[i, k + 1] = (piv[i, k + 1] - piv[i, k] * piv[k + 1, k]) * inv[k + 1]
            for i in range(k + 2, 8):
                for j in range(k + 2, i + 1):
                    piv[i, j] = piv[i, j] - piv[i, k] * piv[j, k] - piv[i, k + 1] * piv[j, k + 1]
        rowv = []
        for i in range(8):
            v = jnp.broadcast_to(tile[i:i + 1, :], (8, lanes))
            for k in range(i):
                v = v - spread(piv[i, k]) * rowv[k]
            rowv.append(v * spread(inv[i]))
        for u in range(t + 1, count):
            cols = []
            acc = tiles[u]
            for i in range(8):
                v = jnp.broadcast_to(tiles[u][:, base + i:base + i + 1], (8, HALF))
                for k in range(i):
                    v = v - piv[i, k] * cols[k]
                cols.append(v * inv[i])
                acc = acc - spread(cols[i]) * rowv[i]
            tiles[u] = acc
        out = rowv[7]
        for i in range(7):
            out = jnp.where(row_at == i, rowv[i], out)
        done.append(out)
    return jnp.concatenate(done, axis=0)


def kernel(data, test, cov_out, factor_out,
           dv, tv, part, sib, q, yrecv, zrecv, ysum, sk, pxr, pzr, cm, am, um, held, root,
           cv, cvb, cxr, czs, czr, zacc,
           ld, xs, xr, ys, yr, zs, zr, sys_, syr, sbs, sbr,
           pxs, pxq, pzs, pzq, pys, pyq, pcs, pcq, cxs, cxq, czs_s, czq):
    x, y, z, c = position()
    zl = lax.rem(z, NZL)
    zh = z // NZL
    o = 1 - c
    nrow, nvar = data.shape
    part_rows = nrow // 2
    sibling = device(x, y, z, o)
    partner = device(x, y, lax.rem(z + NZL, NZ), c)
    far_first = (4, 3, 5, 2, 6, 1, 7)

    def ypeer(k):
        return lax.rem(y + k, NY)

    def zpeer(k):
        return lax.rem(zl + k, NZL)

    def zdev(w):
        return device(x, y, zh * NZL + w, c)

    def xpeer(k):
        return lax.rem(x + k, NX)

    tcopy = pltpu.make_async_copy(test, tv, ld.at[2])
    tcopy.start()

    def dcopy(i):
        at = pl.ds(i * part_rows, part_rows)
        return pltpu.make_async_copy(data.at[at, :], dv.at[at, :], ld.at[i])

    for i in range(2):
        dcopy(i).start()

    barrier = pltpu.get_barrier_semaphore()
    peers = [sibling, partner]
    peers += [device(x, ypeer(k), z, c) for k in range(1, NY)]
    peers += [zdev(zpeer(k)) for k in range(1, NZL)]
    peers += [device(xpeer(k), y, z, c) for k in range(1, NX)]
    for p in peers:
        pl.semaphore_signal(barrier, inc=1, device_id=p, device_id_type=MESH)

    def sib_copy(i):
        at = pl.ds(i * part_rows, part_rows)
        return remote(part.at[o, :, at], sib.at[:, at], xs.at[i], xr.at[i], sibling)

    def y_copy(r):
        return remote(q.at[r], yrecv.at[y], ys.at[r], yr.at[y], device(x, r, z, c))

    tcopy.wait()
    for i in range(2):
        dcopy(i).wait()
        at = slice(i * part_rows, (i + 1) * part_rows)
        p = jnp.dot(dv[at, :], tv[...], preferred_element_type=F32).T
        part[0, :, at] = p[:HALF]
        part[1, :, at] = p[HALF:]
        if i == 0:
            pl.semaphore_wait(barrier, len(peers))
        sib_copy(i).start()
    for i in range(2):
        sib_copy(i).wait_recv()
        at = slice(i * part_rows, (i + 1) * part_rows)
        part[c, :, at] = part[c, :, at] + sib[:, at]
    for k in far_first:
        r = ypeer(k)
        q[r] = encode(part[c, pl.ds(pl.multiple_of(r * BLOCK, BLOCK), BLOCK), :])
        y_copy(r).start()

    total = part[c, pl.ds(pl.multiple_of(y * BLOCK, BLOCK), BLOCK), :]
    for k in range(1, NY):
        r = ypeer(k)
        remote(q.at[r], yrecv.at[r], ys.at[r], yr.at[r], device(x, r, z, c)).wait_recv()
        total = total + decode(yrecv[r])
    q[y] = encode(total)
    z_copy = remote(q.at[y], zrecv, zs, zr, partner)
    z_copy.start()
    z_copy.wait_recv()
    ysum[...] = (decode(q[y]) + decode(zrecv[...])) * (1.0 / K)
    sk[c, y] = ysum[...].astype(BF16)

    def sy_copy(k):
        r = ypeer(k)
        return remote(sk.at[c, y], sk.at[c, y], sys_.at[r], syr.at[y], device(x, r, z, c))

    for k in far_first:
        sy_copy(k).start()
    for k in range(1, NY):
        r = ypeer(k)
        remote(sk.at[c, r], sk.at[c, r], sys_.at[r], syr.at[r], device(x, r, z, c)).wait_recv()
    sb_copy = remote(sk.at[c], sk.at[c], sbs, sbr, sibling)
    sb_copy.start()

    def product(h):
        left = sk[h].reshape(HALF, nrow)

        def tile(j, carry):
            at = pl.ds(pl.multiple_of(j * 1024, 1024), 1024)
            res = jnp.dot(left, dv[:, at], preferred_element_type=F32)
            res = res.reshape(2, NX, BLOCK, 1024)
            cv[pl.ds(2 * h, 2), :, :, at] = res
            cvb[pl.ds(2 * h, 2), :, :, at] = res.astype(BF16)
            return carry

        lax.fori_loop(0, nvar // 1024, tile, 0)

    def cx_copy(w, k):
        r = xpeer(k)
        return remote(cvb.at[w, r], cxr.at[w, x], cxs.at[w, r], cxq.at[w, x], device(r, y, z, c))

    def cz_copy(w):
        return remote(czs.at[w], czr.at[zl], czs_s.at[w], czq.at[zl], zdev(w))

    def x_sum(w):
        for k in range(1, NX):
            r = xpeer(k)
            remote(cvb.at[w, r], cxr.at[w, r], cxs.at[w, r], cxq.at[w, r],
                   device(r, y, z, c)).wait_recv()
        acc = cv[w, x]
        for k in range(1, NX):
            acc = acc + cxr[w, xpeer(k)].astype(F32)

        @pl.when(w == zl)
        def _():
            zacc[...] = acc

        @pl.when(w != zl)
        def _():
            czs[w] = acc.astype(BF16)
            cz_copy(w).start()

    y1 = ysum[...].astype(BF16)
    rest = ysum[...] - y1.astype(F32)
    y2 = rest.astype(BF16)
    y3 = (rest - y2.astype(F32)).astype(BF16)
    left = jnp.concatenate([y1, y2, y3], axis=0)

    def own_rows(h):
        terms = lax.dot_general(left, sk[h].reshape(HALF, nrow), (((1,), (1,)), ((), ())),
                                preferred_element_type=F32)
        terms = (terms[2 * BLOCK:] + terms[BLOCK:2 * BLOCK]) + terms[:BLOCK]
        pxr[x, h] = terms * (1.0 / (NX * NZL * nrow))

    own_rows(c)
    remote(sk.at[o], sk.at[o], sbs, sbr, sibling).wait_recv()
    own_rows(o)

    def px_copy(k):
        r = xpeer(k)
        return remote(pxr.at[x], pxr.at[x], pxs.at[r], pxq.at[x], device(r, y, z, c))

    for k in (2, 1, 3):
        px_copy(k).start()
    product(c)
    for a in range(2):
        for k in (2, 1, 3):
            cx_copy(2 * c + a, k).start()
    product(o)
    for a in range(2):
        for k in (2, 1, 3):
            cx_copy(2 * o + a, k).start()

    for k in range(1, NX):
        r = xpeer(k)
        remote(pxr.at[r], pxr.at[r], pxs.at[r], pxq.at[r], device(r, y, z, c)).wait_recv()
    pzr[zl] = (pxr[0] + pxr[1]) + (pxr[2] + pxr[3])

    def pz_copy(k):
        r = zpeer(k)
        return remote(pzr.at[zl], pzr.at[zl], pzs.at[r], pzq.at[zl], zdev(r))

    for k in (3, 2, 1):
        pz_copy(k).start()
    for k in range(1, NZL):
        r = zpeer(k)
        remote(pzr.at[r], pzr.at[r], pzs.at[r], pzq.at[r], zdev(r)).wait_recv()
    cm[c, y] = (pzr[0] + pzr[1]) + (pzr[2] + pzr[3])

    def py_copy(k):
        r = ypeer(k)
        return remote(cm.at[c, y], cm.at[c, y], pys.at[r], pyq.at[y], device(x, r, z, c))

    for k in far_first:
        py_copy(k).start()
    for a in range(2):
        x_sum(2 * c + a)
    for k in range(1, NY):
        r = ypeer(k)
        remote(cm.at[c, r], cm.at[c, r], pys.at[r], pyq.at[r], device(x, r, z, c)).wait_recv()
    pc_copy = remote(cm.at[c], cm.at[c], pcs, pcq, sibling)
    pc_copy.start()
    remote(cm.at[o], cm.at[o], pcs, pcq, sibling).wait_recv()
    core = jnp.concatenate([cm[:, :, 0].reshape(K, HALF), cm[:, :, 1].reshape(K, HALF)], axis=1)
    core = (core + core.T) * 0.5
    on_diagonal = lax.broadcasted_iota(jnp.int32, (K, K), 0) == lax.broadcasted_iota(jnp.int32, (K, K), 1)
    diagonal = jnp.where(on_diagonal, core, 0.0)
    across = jnp.sum(diagonal, axis=0, keepdims=True)
    root[...] = across * lax.rsqrt(across)
    am[...] = core * lax.rsqrt(jnp.sum(diagonal, axis=1, keepdims=True)) * lax.rsqrt(across)

    lane_at = lax.broadcasted_iota(jnp.int32, (SLAB, K), 1)
    sub_at = lax.broadcasted_iota(jnp.int32, (SLAB, K), 0)

    def slab_step(j, carry):
        start = pl.multiple_of(j * SLAB, SLAB)
        slab = pltpu.roll(am[pl.ds(start, SLAB), :], lax.rem(K - start, K), axis=1)
        u = pltpu.roll(factor_slab(slab, SLAB, K, held), start, axis=1)
        u = jnp.where(lane_at >= sub_at + start, u, 0.0)
        um[pl.ds(start, SLAB), :] = u

        @pl.when(j < K // SLAB - 1)
        def _():
            am[...] -= lax.dot_general(u, u, (((0,), (0,)), ((), ())),
                                       precision=HIGHEST, preferred_element_type=F32)

        @pl.when(j < 2)
        def _():
            x_sum(2 * o + j)

        return carry

    lax.fori_loop(0, K // SLAB, slab_step, 0)
    factor_out[...] = (um[...] * root[...]).T

    acc = zacc[...]
    for k in range(1, NZL):
        r = zpeer(k)
        remote(czs.at[r], czr.at[r], czs_s.at[r], czq.at[r], zdev(r)).wait_recv()
        acc = acc + czr[r].astype(F32)
    cov_out[...] = acc * (1.0 / math.sqrt(NX * NZL * nrow))

    for i in range(2):
        sib_copy(i).wait_send()
    for k in range(1, NY):
        y_copy(ypeer(k)).wait_send()
        sy_copy(k).wait_send()
        py_copy(k).wait_send()
    z_copy.wait_send()
    sb_copy.wait_send()
    for k in range(1, NX):
        px_copy(k).wait_send()
        for w in range(NZL):
            cx_copy(w, k).wait_send()
    pc_copy.wait_send()
    for k in range(1, NZL):
        pz_copy(k).wait_send()
        cz_copy(zpeer(k)).wait_send()


def per_device(data, test_matrix):
    rows_all, nvar = data.shape
    vm = pltpu.VMEM
    dma = pltpu.SemaphoreType.DMA
    scratch = [
        vm((rows_all, nvar), BF16), vm((nvar, K), BF16),
        vm((2, HALF, rows_all), F32), vm((HALF, rows_all), F32),
        vm((NY, BLOCK, rows_all + HALF), BF16), vm((NY, BLOCK, rows_all + HALF), BF16),
        vm((BLOCK, rows_all + HALF), BF16), vm((BLOCK, rows_all), F32),
        vm((2, NY, BLOCK, rows_all), BF16),
        vm((NX, 2, BLOCK, HALF), F32), vm((NZL, 2, BLOCK, HALF), F32), vm((2, NY, 2, BLOCK, HALF), F32),
        vm((K, K), F32), vm((K, K), F32), vm((2, 8, 8, HALF), F32), vm((1, K), F32),
        vm((NZL, NX, BLOCK, nvar), F32), vm((NZL, NX, BLOCK, nvar), BF16),
        vm((NZL, NX, BLOCK, nvar), BF16), vm((NZL, BLOCK, nvar), BF16),
        vm((NZL, BLOCK, nvar), BF16), vm((BLOCK, nvar), F32),
        dma((3,)), dma((2,)), dma((2,)), dma((NY,)), dma((NY,)),
        dma, dma, dma((NY,)), dma((NY,)), dma, dma,
        dma((NX,)), dma((NX,)), dma((NZL,)), dma((NZL,)), dma((NY,)), dma((NY,)),
        dma, dma, dma((NZL, NX)), dma((NZL, NX)), dma((NZL,)), dma((NZL,)),
    ]
    any_ = pl.BlockSpec(memory_space=pl.ANY)
    vmem = pl.BlockSpec(memory_space=pltpu.VMEM)
    cov_t, factor = pl.pallas_call(
        kernel,
        out_shape=(pltpu.VMEM((BLOCK, nvar), F32), pltpu.VMEM((K, K), F32)),
        in_specs=[any_, any_],
        out_specs=(vmem, vmem),
        scratch_shapes=scratch,
        compiler_params=pltpu.CompilerParams(
            collective_id=0, has_side_effects=True, vmem_limit_bytes=62 * 1024 * 1024
        ),
        cost_estimate=pl.CostEstimate(
            flops=4 * rows_all * nvar * K, bytes_accessed=2 * nvar * (rows_all + K),
            transcendentals=0,
        ),
        name="sketch",
    )(data, test_matrix)
    return (cov_t.T, factor)


def solution(mesh):
    return jax.shard_map(
        per_device,
        mesh=mesh,
        in_specs=(P("sample", "var"), P("var", None)),
        out_specs=(P("var", "sample"), P()),
        check_vma=False,
    )
```

```python
import math

import jax
import jax.numpy as jnp
from jax import lax
from jax.experimental import pallas as pl
from jax.experimental.pallas import tpu as pltpu
from jax.sharding import PartitionSpec as P

MESH = pl.DeviceIdType.MESH
HIGHEST = lax.Precision.HIGHEST
F32 = jnp.float32
BF16 = jnp.bfloat16

NX, NY, NZ = 4, 8, 8
NZL = 4
K = 256
HALF = 128
BLOCK = 16
SLAB = 64
SPAN = 83.0
TINY = 1e-30


def position():
    s = lax.axis_index("sample")
    v = lax.axis_index("var")
    x = lax.rem(s, NX)
    zl = s // NX
    c = lax.rem(v, 2)
    zh = lax.rem(v // 2, 2)
    y = v // 4
    return x, y, zh * NZL + zl, c


def device(x, y, z, c):
    return (lax.rem(z, NZL) * NX + x, y * 4 + (z // NZL) * 2 + c)


def remote(src, dst, send, recv, target):
    return pltpu.make_async_remote_copy(
        src_ref=src, dst_ref=dst, send_sem=send, recv_sem=recv,
        device_id=target, device_id_type=MESH,
    )


def encode(a):
    top = jnp.maximum(jnp.max(jnp.abs(a), axis=1, keepdims=True), TINY) * 1.01
    scale = jnp.broadcast_to(top, (a.shape[0], HALF)).astype(BF16)
    wide = jnp.concatenate([SPAN / scale.astype(F32)] * (a.shape[1] // HALF), axis=1)
    return jnp.concatenate([jnp.exp(a * wide).astype(BF16), scale], axis=1)


def decode(e):
    lanes = e.shape[1] - HALF
    scale = e[:, lanes:].astype(F32) * (1.0 / SPAN)
    return jnp.log(e[:, :lanes].astype(F32)) * jnp.concatenate([scale] * (lanes // HALF), axis=1)


def factor_slab(block, rows, lanes, held):
    wide = lanes // HALF

    def spread(a):
        return jnp.concatenate([a] * wide, axis=1)

    count = rows // 8
    tiles = [block[8 * t:8 * t + 8, :] for t in range(count)]
    done = []
    row_at = lax.broadcasted_iota(jnp.int32, (8, lanes), 0)
    for t in range(count):
        tile = tiles[t]
        base = 8 * t
        for j in range(8):
            held[t % 2, j] = jnp.broadcast_to(tile[:, base + j:base + j + 1], (8, HALF))
        piv = {}
        for i in range(8):
            for j in range(i + 1):
                piv[i, j] = jnp.broadcast_to(held[t % 2, j, i:i + 1, :], (8, HALF))
        inv = {}
        for k in range(0, 8, 2):
            first, cross, second = piv[k, k], piv[k + 1, k], piv[k + 1, k + 1]
            root = lax.rsqrt(first)
            inv[k] = root
            inv[k + 1] = lax.rsqrt(first * second - cross * cross) * (first * root)
            piv[k + 1, k] = cross * root
            for i in range(k + 2, 8):
                piv[i, k] = piv[i, k] * root
                piv[i, k + 1] = (piv[i, k + 1] - piv[i, k] * piv[k + 1, k]) * inv[k + 1]
            for i in range(k + 2, 8):
                for j in range(k + 2, i + 1):
                    piv[i, j] = piv[i, j] - piv[i, k] * piv[j, k] - piv[i, k + 1] * piv[j, k + 1]
        rowv = []
        for i in range(8):
            v = jnp.broadcast_to(tile[i:i + 1, :], (8, lanes))
            for k in range(i):
                v = v - spread(piv[i, k]) * rowv[k]
            rowv.append(v * spread(inv[i]))
        for u in range(t + 1, count):
            cols = []
            acc = tiles[u]
            for i in range(8):
                v = jnp.broadcast_to(tiles[u][:, base + i:base + i + 1], (8, HALF))
                for k in range(i):
                    v = v - piv[i, k] * cols[k]
                cols.append(v * inv[i])
                acc = acc - spread(cols[i]) * rowv[i]
            tiles[u] = acc
        out = rowv[7]
        for i in range(7):
            out = jnp.where(row_at == i, rowv[i], out)
        done.append(out)
    return jnp.concatenate(done, axis=0)


def kernel(data, test, cov_out, factor_out,
           dv, tv, part, sib, q, yrecv, zrecv, ysum, sk, pxr, pzr, cm, am, um, held, root,
           cv, cvb, cxr, czs, czr, zacc,
           ld, xs, xr, ys, yr, zs, zr, sys_, syr, sbs, sbr,
           pxs, pxq, pzs, pzq, pys, pyq, pcs, pcq, cxs, cxq, czs_s, czq):
    x, y, z, c = position()
    zl = lax.rem(z, NZL)
    zh = z // NZL
    o = 1 - c
    nrow, nvar = data.shape
    part_rows = nrow // 2
    sibling = device(x, y, z, o)
    partner = device(x, y, lax.rem(z + NZL, NZ), c)
    far_first = (4, 5, 3, 6, 2, 7, 1)

    def ypeer(k):
        return lax.rem(y + k, NY)

    def zpeer(k):
        return lax.rem(zl + k, NZL)

    def zdev(w):
        return device(x, y, zh * NZL + w, c)

    def xpeer(k):
        return lax.rem(x + k, NX)

    tcopy = pltpu.make_async_copy(test, tv, ld.at[2])
    tcopy.start()

    def dcopy(i):
        at = pl.ds(i * part_rows, part_rows)
        return pltpu.make_async_copy(data.at[at, :], dv.at[at, :], ld.at[i])

    for i in range(2):
        dcopy(i).start()

    barrier = pltpu.get_barrier_semaphore()
    peers = [sibling, partner]
    peers += [device(x, ypeer(k), z, c) for k in range(1, NY)]
    peers += [zdev(zpeer(k)) for k in range(1, NZL)]
    peers += [device(xpeer(k), y, z, c) for k in range(1, NX)]
    for p in peers:
        pl.semaphore_signal(barrier, inc=1, device_id=p, device_id_type=MESH)

    def sib_copy(i):
        at = pl.ds(i * part_rows, part_rows)
        return remote(part.at[o, :, at], sib.at[:, at], xs.at[i], xr.at[i], sibling)

    def y_copy(r):
        return remote(q.at[r], yrecv.at[y], ys.at[r], yr.at[y], device(x, r, z, c))

    tcopy.wait()
    for i in range(2):
        dcopy(i).wait()
        at = slice(i * part_rows, (i + 1) * part_rows)
        p = jnp.dot(dv[at, :], tv[...], preferred_element_type=F32).T
        part[0, :, at] = p[:HALF]
        part[1, :, at] = p[HALF:]
        if i == 0:
            pl.semaphore_wait(barrier, len(peers))
        sib_copy(i).start()
    for i in range(2):
        sib_copy(i).wait_recv()
        at = slice(i * part_rows, (i + 1) * part_rows)
        part[c, :, at] = part[c, :, at] + sib[:, at]
    for k in far_first:
        r = ypeer(k)
        q[r] = encode(part[c, pl.ds(pl.multiple_of(r * BLOCK, BLOCK), BLOCK), :])
        y_copy(r).start()

    total = part[c, pl.ds(pl.multiple_of(y * BLOCK, BLOCK), BLOCK), :]
    for k in range(1, NY):
        r = ypeer(k)
        remote(q.at[r], yrecv.at[r], ys.at[r], yr.at[r], device(x, r, z, c)).wait_recv()
        total = total + decode(yrecv[r])
    q[y] = encode(total)
    z_copy = remote(q.at[y], zrecv, zs, zr, partner)
    z_copy.start()
    z_copy.wait_recv()
    ysum[...] = (decode(q[y]) + decode(zrecv[...])) * (1.0 / K)
    sk[c, y] = ysum[...].astype(BF16)

    def sy_copy(k):
        r = ypeer(k)
        return remote(sk.at[c, y], sk.at[c, y], sys_.at[r], syr.at[y], device(x, r, z, c))

    for k in far_first:
        sy_copy(k).start()
    for k in range(1, NY):
        r = ypeer(k)
        remote(sk.at[c, r], sk.at[c, r], sys_.at[r], syr.at[r], device(x, r, z, c)).wait_recv()
    sb_copy = remote(sk.at[c], sk.at[c], sbs, sbr, sibling)
    sb_copy.start()

    def product(h):
        left = sk[h].reshape(HALF, nrow)

        def tile(j, carry):
            at = pl.ds(pl.multiple_of(j * 1024, 1024), 1024)
            res = jnp.dot(left, dv[:, at], preferred_element_type=F32)
            res = res.reshape(2, NX, BLOCK, 1024)
            cv[pl.ds(2 * h, 2), :, :, at] = res
            cvb[pl.ds(2 * h, 2), :, :, at] = res.astype(BF16)
            return carry

        lax.fori_loop(0, nvar // 1024, tile, 0)

    def cx_copy(w, k):
        r = xpeer(k)
        return remote(cvb.at[w, r], cxr.at[w, x], cxs.at[w, r], cxq.at[w, x], device(r, y, z, c))

    def cz_copy(w):
        return remote(czs.at[w], czr.at[zl], czs_s.at[w], czq.at[zl], zdev(w))

    def x_sum(w):
        for k in range(1, NX):
            r = xpeer(k)
            remote(cvb.at[w, r], cxr.at[w, r], cxs.at[w, r], cxq.at[w, r],
                   device(r, y, z, c)).wait_recv()
        acc = cv[w, x]
        for k in range(1, NX):
            acc = acc + cxr[w, xpeer(k)].astype(F32)

        @pl.when(w == zl)
        def _():
            zacc[...] = acc

        @pl.when(w != zl)
        def _():
            czs[w] = acc.astype(BF16)
            cz_copy(w).start()

    y1 = ysum[...].astype(BF16)
    rest = ysum[...] - y1.astype(F32)
    y2 = rest.astype(BF16)
    y3 = (rest - y2.astype(F32)).astype(BF16)
    left = jnp.concatenate([y1, y2, y3], axis=0)

    def own_rows(h):
        terms = lax.dot_general(left, sk[h].reshape(HALF, nrow), (((1,), (1,)), ((), ())),
                                preferred_element_type=F32)
        terms = (terms[2 * BLOCK:] + terms[BLOCK:2 * BLOCK]) + terms[:BLOCK]
        pxr[x, h] = terms * (1.0 / (NX * NZL * nrow))

    own_rows(c)
    remote(sk.at[o], sk.at[o], sbs, sbr, sibling).wait_recv()
    own_rows(o)

    def px_copy(k):
        r = xpeer(k)
        return remote(pxr.at[x], pxr.at[x], pxs.at[r], pxq.at[x], device(r, y, z, c))

    for k in (2, 1, 3):
        px_copy(k).start()
    product(c)
    for a in range(2):
        for k in (2, 1, 3):
            cx_copy(2 * c + a, k).start()
    product(o)
    for a in range(2):
        for k in (2, 1, 3):
            cx_copy(2 * o + a, k).start()

    for k in range(1, NX):
        r = xpeer(k)
        remote(pxr.at[r], pxr.at[r], pxs.at[r], pxq.at[r], device(r, y, z, c)).wait_recv()
    pzr[zl] = (pxr[0] + pxr[1]) + (pxr[2] + pxr[3])

    def pz_copy(k):
        r = zpeer(k)
        return remote(pzr.at[zl], pzr.at[zl], pzs.at[r], pzq.at[zl], zdev(r))

    for k in (3, 2, 1):
        pz_copy(k).start()
    for k in range(1, NZL):
        r = zpeer(k)
        remote(pzr.at[r], pzr.at[r], pzs.at[r], pzq.at[r], zdev(r)).wait_recv()
    cm[c, y] = (pzr[0] + pzr[1]) + (pzr[2] + pzr[3])

    def py_copy(k):
        r = ypeer(k)
        return remote(cm.at[c, y], cm.at[c, y], pys.at[r], pyq.at[y], device(x, r, z, c))

    for k in far_first:
        py_copy(k).start()
    for a in range(2):
        x_sum(2 * c + a)
    for k in range(1, NY):
        r = ypeer(k)
        remote(cm.at[c, r], cm.at[c, r], pys.at[r], pyq.at[r], device(x, r, z, c)).wait_recv()
    pc_copy = remote(cm.at[c], cm.at[c], pcs, pcq, sibling)
    pc_copy.start()
    remote(cm.at[o], cm.at[o], pcs, pcq, sibling).wait_recv()
    core = jnp.concatenate([cm[:, :, 0].reshape(K, HALF), cm[:, :, 1].reshape(K, HALF)], axis=1)
    core = (core + core.T) * 0.5
    on_diagonal = lax.broadcasted_iota(jnp.int32, (K, K), 0) == lax.broadcasted_iota(jnp.int32, (K, K), 1)
    diagonal = jnp.where(on_diagonal, core, 0.0)
    across = jnp.sum(diagonal, axis=0, keepdims=True)
    root[...] = across * lax.rsqrt(across)
    am[...] = core * lax.rsqrt(jnp.sum(diagonal, axis=1, keepdims=True)) * lax.rsqrt(across)

    for j in range(K // SLAB):
        start = j * SLAB
        low = start // HALF * HALF
        wide = K - low
        slab = am[start:start + SLAB, low:]
        if start > low:
            slab = pltpu.roll(slab, wide - (start - low), axis=1)
        u = factor_slab(slab, SLAB, wide, held)
        if start > low:
            u = pltpu.roll(u, start - low, axis=1)
        lane_at = lax.broadcasted_iota(jnp.int32, (SLAB, wide), 1) + low
        sub_at = lax.broadcasted_iota(jnp.int32, (SLAB, wide), 0) + start
        u = jnp.where(lane_at >= sub_at, u, 0.0)
        um[start:start + SLAB, low:] = u
        if low:
            um[start:start + SLAB, :low] = jnp.zeros((SLAB, low), F32)
        if start + SLAB < K:
            update = lax.dot_general(u, u, (((0,), (0,)), ((), ())),
                                     precision=HIGHEST, preferred_element_type=F32)
            am[start + SLAB:, low:] -= update[start + SLAB - low:, :]
        if j < 2:
            x_sum(2 * o + j)

    factor_out[...] = (um[...] * root[...]).T

    acc = zacc[...]
    for k in range(1, NZL):
        r = zpeer(k)
        remote(czs.at[r], czr.at[r], czs_s.at[r], czq.at[r], zdev(r)).wait_recv()
        acc = acc + czr[r].astype(F32)
    cov_out[...] = acc * (1.0 / math.sqrt(NX * NZL * nrow))

    for i in range(2):
        sib_copy(i).wait_send()
    for k in range(1, NY):
        y_copy(ypeer(k)).wait_send()
        sy_copy(k).wait_send()
        py_copy(k).wait_send()
    z_copy.wait_send()
    sb_copy.wait_send()
    for k in range(1, NX):
        px_copy(k).wait_send()
        for w in range(NZL):
            cx_copy(w, k).wait_send()
    pc_copy.wait_send()
    for k in range(1, NZL):
        pz_copy(k).wait_send()
        cz_copy(zpeer(k)).wait_send()


def per_device(data, test_matrix):
    rows_all, nvar = data.shape
    vm = pltpu.VMEM
    dma = pltpu.SemaphoreType.DMA
    scratch = [
        vm((rows_all, nvar), BF16), vm((nvar, K), BF16),
        vm((2, HALF, rows_all), F32), vm((HALF, rows_all), F32),
        vm((NY, BLOCK, rows_all + HALF), BF16), vm((NY, BLOCK, rows_all + HALF), BF16),
        vm((BLOCK, rows_all + HALF), BF16), vm((BLOCK, rows_all), F32),
        vm((2, NY, BLOCK, rows_all), BF16),
        vm((NX, 2, BLOCK, HALF), F32), vm((NZL, 2, BLOCK, HALF), F32), vm((2, NY, 2, BLOCK, HALF), F32),
        vm((K, K), F32), vm((K, K), F32), vm((2, 8, 8, HALF), F32), vm((1, K), F32),
        vm((NZL, NX, BLOCK, nvar), F32), vm((NZL, NX, BLOCK, nvar), BF16),
        vm((NZL, NX, BLOCK, nvar), BF16), vm((NZL, BLOCK, nvar), BF16),
        vm((NZL, BLOCK, nvar), BF16), vm((BLOCK, nvar), F32),
        dma((3,)), dma((2,)), dma((2,)), dma((NY,)), dma((NY,)),
        dma, dma, dma((NY,)), dma((NY,)), dma, dma,
        dma((NX,)), dma((NX,)), dma((NZL,)), dma((NZL,)), dma((NY,)), dma((NY,)),
        dma, dma, dma((NZL, NX)), dma((NZL, NX)), dma((NZL,)), dma((NZL,)),
    ]
    any_ = pl.BlockSpec(memory_space=pl.ANY)
    vmem = pl.BlockSpec(memory_space=pltpu.VMEM)
    cov_t, factor = pl.pallas_call(
        kernel,
        out_shape=(pltpu.VMEM((BLOCK, nvar), F32), pltpu.VMEM((K, K), F32)),
        in_specs=[any_, any_],
        out_specs=(vmem, vmem),
        scratch_shapes=scratch,
        compiler_params=pltpu.CompilerParams(
            collective_id=0, has_side_effects=True, vmem_limit_bytes=62 * 1024 * 1024
        ),
        cost_estimate=pl.CostEstimate(
            flops=4 * rows_all * nvar * K, bytes_accessed=2 * nvar * (rows_all + K),
            transcendentals=0,
        ),
        name="sketch",
    )(data, test_matrix)
    return (cov_t.T, factor)


def solution(mesh):
    return jax.shard_map(
        per_device,
        mesh=mesh,
        in_specs=(P("sample", "var"), P("var", None)),
        out_specs=(P("var", "sample"), P()),
        check_vma=False,
    )
```

```python
import math

import jax
import jax.numpy as jnp
from jax import lax
from jax.experimental import pallas as pl
from jax.experimental.pallas import tpu as pltpu
from jax.sharding import PartitionSpec as P

MESH = pl.DeviceIdType.MESH
HIGHEST = lax.Precision.HIGHEST
F32 = jnp.float32
BF16 = jnp.bfloat16

NX, NY, NZ = 4, 8, 8
NZL = 4
K = 256
HALF = 128
BLOCK = 16
SLAB = 64
SPAN = 83.0
TINY = 1e-30


def position():
    s = lax.axis_index("sample")
    v = lax.axis_index("var")
    x = lax.rem(s, NX)
    zl = s // NX
    c = lax.rem(v, 2)
    zh = lax.rem(v // 2, 2)
    y = v // 4
    return x, y, zh * NZL + zl, c


def device(x, y, z, c):
    return (lax.rem(z, NZL) * NX + x, y * 4 + (z // NZL) * 2 + c)


def remote(src, dst, send, recv, target):
    return pltpu.make_async_remote_copy(
        src_ref=src, dst_ref=dst, send_sem=send, recv_sem=recv,
        device_id=target, device_id_type=MESH,
    )


def encode(a):
    top = jnp.maximum(jnp.max(jnp.abs(a), axis=1, keepdims=True), TINY) * 1.01
    scale = jnp.broadcast_to(top, (a.shape[0], HALF)).astype(BF16)
    wide = jnp.concatenate([SPAN / scale.astype(F32)] * (a.shape[1] // HALF), axis=1)
    return jnp.concatenate([jnp.exp(a * wide).astype(BF16), scale], axis=1)


def decode(e):
    lanes = e.shape[1] - HALF
    scale = e[:, lanes:].astype(F32) * (1.0 / SPAN)
    return jnp.log(e[:, :lanes].astype(F32)) * jnp.concatenate([scale] * (lanes // HALF), axis=1)


def factor_slab(block, rows, lanes, held):
    wide = lanes // HALF

    def spread(a):
        return jnp.concatenate([a] * wide, axis=1)

    count = rows // 8
    tiles = [block[8 * t:8 * t + 8, :] for t in range(count)]
    done = []
    row_at = lax.broadcasted_iota(jnp.int32, (8, lanes), 0)
    for t in range(count):
        tile = tiles[t]
        base = 8 * t
        for j in range(8):
            held[t % 2, j] = jnp.broadcast_to(tile[:, base + j:base + j + 1], (8, HALF))
        piv = {}
        for i in range(8):
            for j in range(i + 1):
                piv[i, j] = jnp.broadcast_to(held[t % 2, j, i:i + 1, :], (8, HALF))
        inv = {}
        for k in range(0, 8, 2):
            first, cross, second = piv[k, k], piv[k + 1, k], piv[k + 1, k + 1]
            root = lax.rsqrt(first)
            inv[k] = root
            inv[k + 1] = lax.rsqrt(first * second - cross * cross) * (first * root)
            piv[k + 1, k] = cross * root
            for i in range(k + 2, 8):
                piv[i, k] = piv[i, k] * root
                piv[i, k + 1] = (piv[i, k + 1] - piv[i, k] * piv[k + 1, k]) * inv[k + 1]
            for i in range(k + 2, 8):
                for j in range(k + 2, i + 1):
                    piv[i, j] = piv[i, j] - piv[i, k] * piv[j, k] - piv[i, k + 1] * piv[j, k + 1]
        rowv = []
        for i in range(8):
            v = jnp.broadcast_to(tile[i:i + 1, :], (8, lanes))
            for k in range(i):
                v = v - spread(piv[i, k]) * rowv[k]
            rowv.append(v * spread(inv[i]))
        for u in range(t + 1, count):
            cols = []
            acc = tiles[u]
            for i in range(8):
                v = jnp.broadcast_to(tiles[u][:, base + i:base + i + 1], (8, HALF))
                for k in range(i):
                    v = v - piv[i, k] * cols[k]
                cols.append(v * inv[i])
                acc = acc - spread(cols[i]) * rowv[i]
            tiles[u] = acc
        out = rowv[7]
        for i in range(7):
            out = jnp.where(row_at == i, rowv[i], out)
        done.append(out)
    return jnp.concatenate(done, axis=0)


def kernel(data, test, cov_out, factor_out,
           dv, tv, part, sib, q, yrecv, zrecv, ysum, sk, pxr, pzr, cm, am, um, held, root,
           cv, cvb, cxr, czs, czr, zacc,
           ld, xs, xr, ys, yr, zs, zr, sys_, syr, sbs, sbr,
           pxs, pxq, pzs, pzq, pys, pyq, pcs, pcq, cxs, cxq, czs_s, czq):
    x, y, z, c = position()
    zl = lax.rem(z, NZL)
    zh = z // NZL
    o = 1 - c
    nrow, nvar = data.shape
    part_rows = nrow // 2
    sibling = device(x, y, z, o)
    partner = device(x, y, lax.rem(z + NZL, NZ), c)
    far_first = (4, 5, 3, 6, 2, 7, 1)

    def ypeer(k):
        return lax.rem(y + k, NY)

    def zpeer(k):
        return lax.rem(zl + k, NZL)

    def zdev(w):
        return device(x, y, zh * NZL + w, c)

    def xpeer(k):
        return lax.rem(x + k, NX)

    tcopy = pltpu.make_async_copy(test, tv, ld.at[2])
    tcopy.start()

    def dcopy(i):
        at = pl.ds(i * part_rows, part_rows)
        return pltpu.make_async_copy(data.at[at, :], dv.at[at, :], ld.at[i])

    for i in range(2):
        dcopy(i).start()

    barrier = pltpu.get_barrier_semaphore()
    peers = [sibling, partner]
    peers += [device(x, ypeer(k), z, c) for k in range(1, NY)]
    peers += [zdev(zpeer(k)) for k in range(1, NZL)]
    peers += [device(xpeer(k), y, z, c) for k in range(1, NX)]
    for p in peers:
        pl.semaphore_signal(barrier, inc=1, device_id=p, device_id_type=MESH)

    def sib_copy(i):
        at = pl.ds(i * part_rows, part_rows)
        return remote(part.at[o, :, at], sib.at[:, at], xs.at[i], xr.at[i], sibling)

    def y_copy(r):
        return remote(q.at[r], yrecv.at[y], ys.at[r], yr.at[y], device(x, r, z, c))

    tcopy.wait()
    for i in range(2):
        dcopy(i).wait()
        at = slice(i * part_rows, (i + 1) * part_rows)
        p = jnp.dot(dv[at, :], tv[...], preferred_element_type=F32).T
        part[0, :, at] = p[:HALF]
        part[1, :, at] = p[HALF:]
        if i == 0:
            pl.semaphore_wait(barrier, len(peers))
        sib_copy(i).start()
    for i in range(2):
        sib_copy(i).wait_recv()
        at = slice(i * part_rows, (i + 1) * part_rows)
        part[c, :, at] = part[c, :, at] + sib[:, at]
    for k in far_first:
        r = ypeer(k)
        q[r] = encode(part[c, pl.ds(pl.multiple_of(r * BLOCK, BLOCK), BLOCK), :])
        y_copy(r).start()

    total = part[c, pl.ds(pl.multiple_of(y * BLOCK, BLOCK), BLOCK), :]
    for k in reversed(far_first):
        r = ypeer(k)
        remote(q.at[r], yrecv.at[r], ys.at[r], yr.at[r], device(x, r, z, c)).wait_recv()
        total = total + decode(yrecv[r])
    q[y] = encode(total)
    z_copy = remote(q.at[y], zrecv, zs, zr, partner)
    z_copy.start()
    z_copy.wait_recv()
    ysum[...] = (decode(q[y]) + decode(zrecv[...])) * (1.0 / K)
    sk[c, y] = ysum[...].astype(BF16)

    def sy_copy(k):
        r = ypeer(k)
        return remote(sk.at[c, y], sk.at[c, y], sys_.at[r], syr.at[y], device(x, r, z, c))

    for k in far_first:
        sy_copy(k).start()
    for k in range(1, NY):
        r = ypeer(k)
        remote(sk.at[c, r], sk.at[c, r], sys_.at[r], syr.at[r], device(x, r, z, c)).wait_recv()
    sb_copy = remote(sk.at[c], sk.at[c], sbs, sbr, sibling)
    sb_copy.start()

    def product(h):
        left = sk[h].reshape(HALF, nrow)

        def tile(j, carry):
            at = pl.ds(pl.multiple_of(j * 1024, 1024), 1024)
            res = jnp.dot(left, dv[:, at], preferred_element_type=F32)
            res = res.reshape(2, NX, BLOCK, 1024)
            cv[pl.ds(2 * h, 2), :, :, at] = res
            cvb[pl.ds(2 * h, 2), :, :, at] = res.astype(BF16)
            return carry

        lax.fori_loop(0, nvar // 1024, tile, 0)

    def cx_copy(w, k):
        r = xpeer(k)
        return remote(cvb.at[w, r], cxr.at[w, x], cxs.at[w, r], cxq.at[w, x], device(r, y, z, c))

    def cz_copy(w):
        return remote(czs.at[w], czr.at[zl], czs_s.at[w], czq.at[zl], zdev(w))

    def x_sum(w):
        for k in range(1, NX):
            r = xpeer(k)
            remote(cvb.at[w, r], cxr.at[w, r], cxs.at[w, r], cxq.at[w, r],
                   device(r, y, z, c)).wait_recv()
        acc = cv[w, x]
        for k in range(1, NX):
            acc = acc + cxr[w, xpeer(k)].astype(F32)

        @pl.when(w == zl)
        def _():
            zacc[...] = acc

        @pl.when(w != zl)
        def _():
            czs[w] = acc.astype(BF16)
            cz_copy(w).start()

    y1 = ysum[...].astype(BF16)
    rest = ysum[...] - y1.astype(F32)
    y2 = rest.astype(BF16)
    y3 = (rest - y2.astype(F32)).astype(BF16)
    left = jnp.concatenate([y1, y2, y3], axis=0)

    def own_rows(h):
        terms = lax.dot_general(left, sk[h].reshape(HALF, nrow), (((1,), (1,)), ((), ())),
                                preferred_element_type=F32)
        terms = (terms[2 * BLOCK:] + terms[BLOCK:2 * BLOCK]) + terms[:BLOCK]
        pxr[x, h] = terms * (1.0 / (NX * NZL * nrow))

    own_rows(c)
    remote(sk.at[o], sk.at[o], sbs, sbr, sibling).wait_recv()
    own_rows(o)

    def px_copy(k):
        r = xpeer(k)
        return remote(pxr.at[x], pxr.at[x], pxs.at[r], pxq.at[x], device(r, y, z, c))

    for k in (2, 1, 3):
        px_copy(k).start()
    product(c)
    for a in range(2):
        for k in (2, 1, 3):
            cx_copy(2 * c + a, k).start()
    product(o)
    for a in range(2):
        for k in (2, 1, 3):
            cx_copy(2 * o + a, k).start()

    for k in range(1, NX):
        r = xpeer(k)
        remote(pxr.at[r], pxr.at[r], pxs.at[r], pxq.at[r], device(r, y, z, c)).wait_recv()
    pzr[zl] = (pxr[0] + pxr[1]) + (pxr[2] + pxr[3])

    def pz_copy(k):
        r = zpeer(k)
        return remote(pzr.at[zl], pzr.at[zl], pzs.at[r], pzq.at[zl], zdev(r))

    for k in (3, 2, 1):
        pz_copy(k).start()
    for k in range(1, NZL):
        r = zpeer(k)
        remote(pzr.at[r], pzr.at[r], pzs.at[r], pzq.at[r], zdev(r)).wait_recv()
    cm[c, y] = (pzr[0] + pzr[1]) + (pzr[2] + pzr[3])

    def py_copy(k):
        r = ypeer(k)
        return remote(cm.at[c, y], cm.at[c, y], pys.at[r], pyq.at[y], device(x, r, z, c))

    for k in far_first:
        py_copy(k).start()
    x_sum(2 * c)
    for k in range(1, NY):
        r = ypeer(k)
        remote(cm.at[c, r], cm.at[c, r], pys.at[r], pyq.at[r], device(x, r, z, c)).wait_recv()
    pc_copy = remote(cm.at[c], cm.at[c], pcs, pcq, sibling)
    pc_copy.start()
    remote(cm.at[o], cm.at[o], pcs, pcq, sibling).wait_recv()
    core = jnp.concatenate([cm[:, :, 0].reshape(K, HALF), cm[:, :, 1].reshape(K, HALF)], axis=1)
    core = (core + core.T) * 0.5
    on_diagonal = lax.broadcasted_iota(jnp.int32, (K, K), 0) == lax.broadcasted_iota(jnp.int32, (K, K), 1)
    diagonal = jnp.where(on_diagonal, core, 0.0)
    across = jnp.sum(diagonal, axis=0, keepdims=True)
    root[...] = across * lax.rsqrt(across)
    am[...] = core * lax.rsqrt(jnp.sum(diagonal, axis=1, keepdims=True)) * lax.rsqrt(across)

    for j in range(K // SLAB):
        start = j * SLAB
        low = start // HALF * HALF
        wide = K - low
        slab = am[start:start + SLAB, low:]
        if start > low:
            slab = pltpu.roll(slab, wide - (start - low), axis=1)
        u = factor_slab(slab, SLAB, wide, held)
        if start > low:
            u = pltpu.roll(u, start - low, axis=1)
        lane_at = lax.broadcasted_iota(jnp.int32, (SLAB, wide), 1) + low
        sub_at = lax.broadcasted_iota(jnp.int32, (SLAB, wide), 0) + start
        u = jnp.where(lane_at >= sub_at, u, 0.0)
        um[start:start + SLAB, low:] = u
        if low:
            um[start:start + SLAB, :low] = jnp.zeros((SLAB, low), F32)
        if start + SLAB < K:
            update = lax.dot_general(u, u, (((0,), (0,)), ((), ())),
                                     precision=HIGHEST, preferred_element_type=F32)
            am[start + SLAB:, low:] -= update[start + SLAB - low:, :]
        if j == 0:
            x_sum(2 * c + 1)
            x_sum(2 * o)
        if j == 1:
            x_sum(2 * o + 1)

    factor_out[...] = (um[...] * root[...]).T

    acc = zacc[...]
    for k in range(1, NZL):
        r = zpeer(k)
        remote(czs.at[r], czr.at[r], czs_s.at[r], czq.at[r], zdev(r)).wait_recv()
        acc = acc + czr[r].astype(F32)
    cov_out[...] = acc * (1.0 / math.sqrt(NX * NZL * nrow))

    for i in range(2):
        sib_copy(i).wait_send()
    for k in range(1, NY):
        y_copy(ypeer(k)).wait_send()
        sy_copy(k).wait_send()
        py_copy(k).wait_send()
    z_copy.wait_send()
    sb_copy.wait_send()
    for k in range(1, NX):
        px_copy(k).wait_send()
        for w in range(NZL):
            cx_copy(w, k).wait_send()
    pc_copy.wait_send()
    for k in range(1, NZL):
        pz_copy(k).wait_send()
        cz_copy(zpeer(k)).wait_send()


def per_device(data, test_matrix):
    rows_all, nvar = data.shape
    vm = pltpu.VMEM
    dma = pltpu.SemaphoreType.DMA
    scratch = [
        vm((rows_all, nvar), BF16), vm((nvar, K), BF16),
        vm((2, HALF, rows_all), F32), vm((HALF, rows_all), F32),
        vm((NY, BLOCK, rows_all + HALF), BF16), vm((NY, BLOCK, rows_all + HALF), BF16),
        vm((BLOCK, rows_all + HALF), BF16), vm((BLOCK, rows_all), F32),
        vm((2, NY, BLOCK, rows_all), BF16),
        vm((NX, 2, BLOCK, HALF), F32), vm((NZL, 2, BLOCK, HALF), F32), vm((2, NY, 2, BLOCK, HALF), F32),
        vm((K, K), F32), vm((K, K), F32), vm((2, 8, 8, HALF), F32), vm((1, K), F32),
        vm((NZL, NX, BLOCK, nvar), F32), vm((NZL, NX, BLOCK, nvar), BF16),
        vm((NZL, NX, BLOCK, nvar), BF16), vm((NZL, BLOCK, nvar), BF16),
        vm((NZL, BLOCK, nvar), BF16), vm((BLOCK, nvar), F32),
        dma((3,)), dma((2,)), dma((2,)), dma((NY,)), dma((NY,)),
        dma, dma, dma((NY,)), dma((NY,)), dma, dma,
        dma((NX,)), dma((NX,)), dma((NZL,)), dma((NZL,)), dma((NY,)), dma((NY,)),
        dma, dma, dma((NZL, NX)), dma((NZL, NX)), dma((NZL,)), dma((NZL,)),
    ]
    any_ = pl.BlockSpec(memory_space=pl.ANY)
    vmem = pl.BlockSpec(memory_space=pltpu.VMEM)
    cov_t, factor = pl.pallas_call(
        kernel,
        out_shape=(pltpu.VMEM((BLOCK, nvar), F32), pltpu.VMEM((K, K), F32)),
        in_specs=[any_, any_],
        out_specs=(vmem, vmem),
        scratch_shapes=scratch,
        compiler_params=pltpu.CompilerParams(
            collective_id=0, has_side_effects=True, vmem_limit_bytes=62 * 1024 * 1024
        ),
        cost_estimate=pl.CostEstimate(
            flops=4 * rows_all * nvar * K, bytes_accessed=2 * nvar * (rows_all + K),
            transcendentals=0,
        ),
        name="sketch",
    )(data, test_matrix)
    return (cov_t.T, factor)


def solution(mesh):
    return jax.shard_map(
        per_device,
        mesh=mesh,
        in_specs=(P("sample", "var"), P("var", None)),
        out_specs=(P("var", "sample"), P()),
        check_vma=False,
    )
```
